128 devices in a mesh: group: 4 (over y), rank: 32 (over z, x, core).
Axes of the slice: x: 4, y: 4, z: 4, core: 2. Of those that a mesh axis runs over, the one named last changes fastest.
Arguments:
- local_grads: bfloat16 [4, 32, 256, 8192], P('group', 'rank'), may hold values from -1 to 1
- master: float32 [256, 8192], P(('group', 'rank')), may hold values from -3 to 3
- first_moment: float32 [256, 8192], P(('group', 'rank')), may hold values from -3 to 3
- second_moment: float32 [256, 8192], P(('group', 'rank')), may hold values from 0.05 to 2
- new_owner: int32 [64], replicated, may hold values from 0 to 95, as said below
Outputs:
- weights: bfloat16 [256, 8192], replicated
- kept_state: float32 [256, 3, 8192], P(('group', 'rank'))
- adopted_state: float32 [4, 32, 2, 3, 8192], P('group', 'rank')
The draws below stay inside these ranges and needn't reach their ends.
Inputs may be any that keep to these rules, and one draw needn't show every extreme that they name: new_owner[j] numbers a surviving device as group * 32 + rank. No surviving device adopts more than 2 rows, and in every draw some device adopts exactly 2.
All inputs are finite; a program needn't handle non-finite values.
Results may differ from the reference program's by a relative error of at most 0.003.
Values may be sent and summed in bfloat16 or wider, within the bound.
No kernel may reach another device: no remote copies, remote signals or barrier semaphores. Data moves between devices by JAX's collectives and lax.ppermute only.
A program may use at most 64 MiB of HBM per device.

```python
import math
import jax
import jax.numpy as jnp
from jax import lax

D = 8192
ROWS_PER_HOLDER = 2
ADAM_STEP = 20
ROWS = 256
N_GROUP = 4
N_RANK = 32


def draw_new_owner(key, part):
    key = jax.random.fold_in(key, 11)
    initial_key, candidate_key, key_order = jax.random.split(key, 3)
    remaining_groups = (N_GROUP - 1) * N_RANK
    leaving_rows = N_RANK * ROWS_PER_HOLDER
    picked_owner = jax.random.randint(initial_key, (), 0, remaining_groups).astype(jnp.int32)
    candidate_owners = jax.random.permutation(candidate_key, (remaining_groups - 1) * ROWS_PER_HOLDER).astype(jnp.int32)
    others = candidate_owners[:leaving_rows - ROWS_PER_HOLDER] // ROWS_PER_HOLDER
    others = others + (others >= picked_owner).astype(jnp.int32)
    busiest = jnp.zeros((ROWS_PER_HOLDER,), jnp.int32) + picked_owner
    owners = jnp.concatenate([busiest, others], axis=0)
    order = jax.random.permutation(key_order, leaving_rows).astype(jnp.int32)
    return owners[order].astype(jnp.int32)


def with_spikes(entries, key, source, target, parts, factor):
    def block_of(position):
        return (jnp.arange(entries.shape[position]) // (entries.shape[position] // parts)).reshape((-1,) + (1,) * (entries.ndim - 1 - position))

    near = jax.random.permutation(key, parts)[block_of(target)]
    far = (block_of(target) + parts // 2) % parts
    return jnp.where((block_of(source) == near) | (block_of(source) == far), factor * entries, entries)


def steps_of(rng, dims, pieces, low, high):
    def one(axis_at, blocks):
        draws = jax.random.uniform(jax.random.fold_in(jax.random.fold_in(rng, 6), axis_at), (blocks,), jnp.float32, low / len(pieces), high / len(pieces))
        return jnp.repeat(jnp.exp(draws), dims[axis_at] // blocks).reshape((-1,) + (1,) * (len(dims) - axis_at - 1))

    level = one(*pieces[0])
    for cut in pieces[1:]:
        level = level * one(*cut)
    return level


def normal_values(stream_key, extent, deviation, limit, cuts=(), kind=jnp.bfloat16):
    loudness = steps_of(stream_key, extent, cuts, -0.22, 0.18) if cuts else 1.0
    array = jax.random.normal(stream_key, extent, jnp.float32) * deviation * loudness
    return jnp.minimum(jnp.maximum(array, -limit), limit).astype(kind)


def heavy_noise(own_key, shape, scale, limit, pieces, heavy, held_as=jnp.bfloat16):
    entries = scale * jax.random.normal(own_key, shape, jnp.float32)
    if pieces:
        entries = entries * steps_of(own_key, shape, pieces, -0.22, 0.18)
    return jnp.clip(with_spikes(entries, jax.random.fold_in(own_key, 3), *heavy), -limit, limit).astype(held_as)


def setup_inputs(seed: int = 0) -> dict:
    key_of = jax.random.split(jax.random.key(seed), 6)
    local_grads = heavy_noise(key_of[0], (N_GROUP, N_RANK, ROWS, D), ((N_GROUP * N_RANK) ** -0.5), 1.0, ((0, 4), (1, 32)), (1, 2, 32, 2.75))
    master = normal_values(key_of[1], (ROWS, D), 0.5, 3.0, ((0, 128),), jnp.float32)
    first_moment = normal_values(key_of[2], (ROWS, D), 0.5, 3.0, ((0, 128),), jnp.float32)
    second_moment = jnp.clip(jnp.exp(math.log(2.0) - 3.6888794 * jax.random.uniform(key_of[3], (ROWS, D), jnp.float32) ** steps_of(key_of[3], (ROWS, D), ((0, 128),), -0.2, 0.2)), 0.05, 2.0)
    new_owner = draw_new_owner(jax.random.fold_in(key_of[5], 71), 0)
    return {"local_grads": local_grads, "master": master, "first_moment": first_moment, "second_moment": second_moment, "new_owner": new_owner}


beta_one = 0.9
beta_two = 0.95
learn_rate = 0.05
epsilon = 1e-08

def adam_update(master, first, second, gradient):
    first_new = beta_one * first + (1.0 - beta_one) * gradient
    second_new = beta_two * second + (1.0 - beta_two) * gradient * gradient
    corr_one = 1.0 - beta_one ** ADAM_STEP
    corr_two = 1.0 - beta_two ** ADAM_STEP
    master_new = master - learn_rate * (first_new / corr_one) / (jnp.sqrt(second_new / corr_two) + epsilon)
    return (master_new, first_new, second_new)

def adoption_slots(new_owner):
    number = new_owner.shape[0]
    same_owner = new_owner[:, None] == new_owner[None, :]
    earlier = lax.broadcasted_iota(jnp.int32, (number, number), 1) < lax.broadcasted_iota(jnp.int32, (number, number), 0)
    return lax.optimization_barrier(jnp.sum((same_owner & earlier).astype(jnp.int32), axis=1)).astype(jnp.int32)

def add_device(running, device_term):
    return (running + device_term.astype(jnp.float32), None)

def reference(local_grads, master, first_moment, second_moment, new_owner):
    per_device = local_grads.reshape(N_GROUP * N_RANK, ROWS, D)
    gradient = lax.scan(add_device, jnp.zeros((ROWS, D), jnp.float32), per_device)[0]
    master_new, first_new, second_new = adam_update(master, first_moment, second_moment, gradient)
    weights = master_new.astype(jnp.bfloat16)
    new_state = jnp.stack([master_new, first_new, second_new], axis=1)
    surviving_rows = (N_GROUP - 1) * N_RANK * ROWS_PER_HOLDER
    row_ids = jnp.arange(ROWS)
    kept_state = jnp.where((row_ids < surviving_rows)[:, None, None], new_state, jnp.zeros_like(new_state))
    slot_index = adoption_slots(new_owner)
    target = (new_owner * ROWS_PER_HOLDER + slot_index).astype(jnp.int32)
    leaving_state = new_state[surviving_rows:]
    adopted = jnp.zeros((N_GROUP * N_RANK * ROWS_PER_HOLDER, 3, D), jnp.float32).at[target].set(leaving_state)
    adopted_state = adopted.reshape(N_GROUP, N_RANK, ROWS_PER_HOLDER, 3, D)
    return (weights, kept_state, adopted_state)
```

```python
import functools

import jax
import jax.numpy as jnp
from jax import lax
from jax.experimental import pallas as pl
from jax.experimental.pallas import tpu as pltpu
from jax.sharding import Mesh
from jax.sharding import PartitionSpec as P

ADAM_STEP = 20

beta_one = 0.9
beta_two = 0.95
learn_rate = 0.05
epsilon = 1e-08

CHIPS = ("y", "z", "x")
BF = jnp.bfloat16
F32 = jnp.float32


def adam_update(master, first, second, gradient):
    first_new = beta_one * first + (1.0 - beta_one) * gradient
    second_new = beta_two * second + (1.0 - beta_two) * gradient * gradient
    corr_one = 1.0 - beta_one**ADAM_STEP
    corr_two = 1.0 - beta_two**ADAM_STEP
    master_new = master - learn_rate * (first_new / corr_one) / (
        jnp.sqrt(second_new / corr_two) + epsilon
    )
    return (master_new, first_new, second_new)


def iota(shape, dim):
    return lax.broadcasted_iota(jnp.int32, shape, dim)


def one_hot(target, columns):
    return jnp.where(iota(target.shape, 1) == target, 1.0, 0.0).astype(BF)


def pick(matrix, values):
    return jnp.dot(matrix, values, preferred_element_type=F32)


def kept_blocks(rows, core):
    stacked = jnp.concatenate([rows[:, k * 1024 : (k + 1) * 1024] for k in range(8)], axis=0)
    p = iota((128, 256), 0)
    target = ((p >> 1) & 7) * 32 + (p >> 4) * 4 + 2 * core + (p & 1)
    return pick(one_hot(target, 256), stacked)


def leaving_rows(rows):
    n = iota((64, 64), 0)
    return pick(one_hot(2 * (n & 31) + (n >> 5), 64), rows)


def send_kernel(kept_ref, leave_ref, master_ref, first_ref, second_ref, out_ref, state_ref, rows_ref):
    step = pl.program_id(0)
    core = 1 - lax.axis_index("core")

    @pl.when(step == 0)
    def _():
        rows_ref[...] = jnp.zeros_like(rows_ref)
        rows_ref[0:2, :] = master_ref[...]
        rows_ref[2:4, :] = first_ref[...]
        rows_ref[4:6, :] = second_ref[...]
        for t in range(32):
            for h in range(2):
                state_ref[t, 8 * h : 8 * h + 8, :] = rows_ref[:, t * 256 + h * 128 : t * 256 + (h + 1) * 128]

    @pl.when(step < 6)
    def _():
        blocks = kept_blocks(kept_ref[...], core).astype(BF)
        out_ref[...] = blocks.reshape(8, 16, 1024)

    @pl.when(step >= 6)
    def _():
        rows = leaving_rows(leave_ref[...])
        for q in range(8):
            mine = jnp.where(
                core == 0, rows[:, q * 512 : q * 512 + 256], rows[:, q * 512 + 256 : q * 512 + 512]
            ).astype(BF)
            for a in range(4):
                out_ref[q, :, a * 256 : (a + 1) * 256] = mine[16 * a : 16 * a + 16, :]


def add_kernel(kept_ref, leave_ref, got_ref, out_ref):
    step = pl.program_id(0)
    core = lax.axis_index("core")

    @pl.when(step < 6)
    def _():
        got = got_ref[...].reshape(128, 1024).astype(F32)
        out_ref[...] = (kept_blocks(kept_ref[...], core) + got).astype(BF).reshape(8, 16, 1024)

    @pl.when(step >= 6)
    def _():
        rows = leaving_rows(leave_ref[...])
        for q in range(8):
            mine = jnp.where(
                core == 0, rows[:, q * 512 : q * 512 + 256], rows[:, q * 512 + 256 : q * 512 + 512]
            )
            for a in range(4):
                cut = slice(a * 256, (a + 1) * 256)
                got = got_ref[q, :, cut].astype(F32)
                out_ref[q, :, cut] = (mine[16 * a : 16 * a + 16, :] + got).astype(BF)


def adam_kernel(parts_ref, master_ref, first_ref, second_ref, state_ref, key_ref, kept_ref, out_ref, old_ref):
    leaving = lax.axis_index("y") == 3

    def add(d, total):
        return total + parts_ref[d].astype(F32)

    gradient = lax.fori_loop(1, 64, add, parts_ref[0].astype(F32), unroll=7)

    @pl.when(leaving)
    def _():
        for i in range(3):
            for a in range(4):
                for h in range(2):
                    start = 256 * (a % 2) + 8 * h + 2 * i + a // 2
                    at = a * 256 + h * 128
                    old_ref[i, :, at : at + 128] = state_ref[pl.ds(start, 16, stride=16), :]

    @pl.when(jnp.logical_not(leaving))
    def _():
        for i, ref in enumerate((master_ref, first_ref, second_ref)):
            for k in range(8):
                old_ref[i, 2 * k : 2 * k + 2, :] = ref[:, k * 1024 : (k + 1) * 1024]

    new = adam_update(old_ref[0], old_ref[1], old_ref[2], gradient)
    for i in range(3):
        value = jnp.where(leaving, jnp.zeros_like(new[i]), new[i])
        for k in range(8):
            for r in range(2):
                kept_ref[r, i : i + 1, k * 1024 : (k + 1) * 1024] = value[2 * k + r : 2 * k + r + 1, :]

    weights = new[0].astype(BF)

    def spread(d, carry):
        out_ref[d, :, 0:1024] = weights
        return carry

    lax.fori_loop(0, 64, spread, 0, unroll=8)

    moments = jnp.concatenate(
        [
            new[1 + part // 2][:, a * 256 + (part % 2) * 128 : a * 256 + (part % 2) * 128 + 128]
            for part in range(4)
            for a in range(4)
        ],
        axis=0,
    ).astype(BF)
    p = iota((1024, 256), 0)
    wanted = (p >> 4) * 4 + (p & 3) + 512 * ((p >> 2) & 3)
    chosen = jnp.where(key_ref[0:1, :] == wanted, 1.0, 0.0).astype(BF)
    out_ref[:, :, 1024:1152] = pick(chosen, moments).astype(BF).reshape(64, 16, 128)


def place_kernel(
    own_ref, other_ref, own_left_ref, other_left_ref, key_ref, weights_ref, adopted_ref, rows_ref, state_ref
):
    step = pl.program_id(0)
    core = lax.axis_index("core")
    chip = (lax.axis_index("y") * 4 + lax.axis_index("z")) * 4 + lax.axis_index("x")

    @pl.when(step < 6)
    def _():
        stacked = jnp.concatenate(
            [own_ref[:, :, 0:1024].reshape(128, 1024), other_ref[:, :, 0:1024].reshape(128, 1024)], axis=0
        )
        p = iota((256, 256), 0)
        row = p & 31
        half = jnp.where(((row >> 1) & 1) == core, 0, 128)
        target = half + (row >> 2) * 16 + (p >> 5) * 2 + (row & 1)
        rows = pick(one_hot(target, 256), stacked).astype(BF)
        for k in range(8):
            weights_ref[:, k * 1024 : (k + 1) * 1024] = rows[32 * k : 32 * k + 32, :]

    for h in range(2):

        @pl.when(step == 6 + h)
        def _():
            for q in range(16):
                for ref, side in ((own_left_ref, core), (other_left_ref, 1 - core)):
                    at = pl.ds(pl.multiple_of((2 * q + side) * 256, 256), 256)
                    for r in range(2):
                        a = 2 * r + h
                        rows_ref[16 * r : 16 * r + 16, at] = ref[q, :, a * 256 : (a + 1) * 256]
            rows = rows_ref[...]
            n = iota((32, 32), 0)
            weights_ref[...] = pick(one_hot((n & 1) * 16 + (n >> 1), 32), rows).astype(BF)
            k = iota((8, 32), 0)
            wanted = jnp.where(k < 2, chip * 4 + core * 2 + k, -1)
            chosen = jnp.where(key_ref[1 + h : 2 + h, 0:32] == wanted, 1.0, 0.0).astype(BF)
            masters = pick(chosen, rows)
            if h == 0:
                state_ref[...] = masters
                for ref, side in ((own_left_ref, core), (other_left_ref, 1 - core)):
                    moments = jnp.concatenate([ref[q, :, 1024:1152] for q in range(16)], axis=1)
                    for low in range(2):
                        k = iota((8, 16), 0)
                        target = jnp.where(
                            (k >= 2) & (k < 6), (((k >> 1) - 1) * 2 + low) * 4 + core * 2 + (k & 1), -1
                        )
                        found = pick(one_hot(target, 16), moments)
                        for q in range(16):
                            at = pl.ds(pl.multiple_of((2 * q + side) * 256 + low * 128, 128), 128)
                            state_ref[:, at] += found[:, q * 128 : (q + 1) * 128]
            else:
                state_ref[...] += masters
                for i in range(3):
                    for slot in range(2):
                        adopted_ref[slot, i : i + 1, :] = state_ref[2 * i + slot : 2 * i + slot + 1, :]


def adoption_keys(new_owner):
    number = new_owner.shape[0]
    same_owner = new_owner[:, None] == new_owner[None, :]
    earlier = iota((number, number), 1) < iota((number, number), 0)
    slot = jnp.sum((same_owner & earlier).astype(jnp.int32), axis=1)
    key = (new_owner * 2 + slot).reshape(32, 2).T
    halves = key.reshape(2, 2, 16).transpose(1, 0, 2).reshape(2, 32)
    quarters = (key.reshape(1, 64) + 512 * jnp.arange(4, dtype=jnp.int32)[:, None]).reshape(1, 256)
    return jnp.concatenate([quarters, jnp.pad(halves, ((0, 5), (0, 224)), constant_values=-1)], axis=0)


def params():
    return pltpu.CompilerParams(vmem_limit_bytes=48 * 1024 * 1024)


def body(local_grads, master, first, second, new_owner):
    grads = local_grads.reshape(256, 8192)
    keys = adoption_keys(new_owner)
    kept_spec = pl.BlockSpec((32, 8192), lambda i: (jnp.minimum(i, 5), 0))
    leave_spec = pl.BlockSpec((64, 4096), lambda i: (3, jnp.maximum(i - 6, 0)))
    block_spec = pl.BlockSpec((8, 16, 1024), lambda i: (i, 0, 0))
    state_spec = pl.BlockSpec((2, 8192), lambda i: (0, 0))
    blocks = jax.ShapeDtypeStruct((64, 16, 1024), BF)
    to_send, state = pl.pallas_call(
        send_kernel,
        grid=(8,),
        in_specs=[kept_spec, leave_spec, state_spec, state_spec, state_spec],
        out_specs=[block_spec, pl.BlockSpec((32, 16, 128), lambda i: (0, 0, 0))],
        out_shape=[blocks, jax.ShapeDtypeStruct((32, 16, 128), F32)],
        scratch_shapes=[pltpu.VMEM((8, 8192), F32)],
        compiler_params=params(),
        name="send_blocks",
    )(grads, grads, master, first, second)
    swap = [(0, 1), (1, 0)]
    got = lax.ppermute(to_send, "core", swap)
    state = lax.all_to_all(state, ("z", "x", "core"), 0, 0, tiled=True)
    partial = pl.pallas_call(
        add_kernel,
        grid=(8,),
        in_specs=[kept_spec, leave_spec, block_spec],
        out_specs=block_spec,
        out_shape=blocks,
        compiler_params=params(),
        name="add_blocks",
    )(grads, grads, got)
    partial = lax.all_to_all(partial, CHIPS, 0, 0, tiled=True)
    kept, payload = pl.pallas_call(
        adam_kernel,
        out_shape=[
            jax.ShapeDtypeStruct((2, 3, 8192), F32),
            jax.ShapeDtypeStruct((64, 16, 1152), BF),
        ],
        scratch_shapes=[pltpu.VMEM((3, 16, 1024), F32)],
        compiler_params=params(),
        name="adam",
    )(partial, master, first, second, state.reshape(512, 128), keys)
    own = lax.all_to_all(payload, CHIPS, 0, 0, tiled=True)
    other = lax.ppermute(own, "core", swap)
    group_spec = pl.BlockSpec((8, 16, 1152), lambda i: (jnp.minimum(i, 5), 0, 0))
    left_spec = pl.BlockSpec((16, 16, 1152), lambda i: (3, 0, 0))
    weights, adopted = pl.pallas_call(
        place_kernel,
        grid=(8,),
        in_specs=[group_spec, group_spec, left_spec, left_spec, pl.BlockSpec((8, 256), lambda i: (0, 0))],
        out_specs=[
            pl.BlockSpec((32, 8192), lambda i: (i, 0)),
            pl.BlockSpec((2, 3, 8192), lambda i: (0, 0, 0)),
        ],
        out_shape=[
            jax.ShapeDtypeStruct((256, 8192), BF),
            jax.ShapeDtypeStruct((2, 3, 8192), F32),
        ],
        scratch_shapes=[pltpu.VMEM((32, 8192), BF), pltpu.VMEM((8, 8192), F32)],
        compiler_params=params(),
        name="place",
    )(own, other, own, other, keys)
    return (weights, kept, adopted[None, None])


def solution(mesh):
    fine = Mesh(mesh.devices.reshape(4, 4, 4, 2), ("y", "z", "x", "core"))
    every = ("y", "z", "x", "core")
    in_specs = (P("y", ("z", "x", "core"), None, None), P(every, None), P(every, None), P(every, None), P())
    out_specs = (P(), P(every, None, None), P("y", ("z", "x", "core"), None, None, None))
    return jax.shard_map(body, mesh=fine, in_specs=in_specs, out_specs=out_specs, check_vma=False)
```

```python
import jax
import jax.numpy as jnp
from jax import lax
from jax.experimental import pallas as pl
from jax.experimental.pallas import tpu as pltpu
from jax.sharding import Mesh
from jax.sharding import PartitionSpec as P

ADAM_STEP = 20

beta_one = 0.9
beta_two = 0.95
learn_rate = 0.05
epsilon = 1e-08

CHIPS = ("y", "z", "x")
BF = jnp.bfloat16
F32 = jnp.float32
HALF = 4096


def adam_update(master, first, second, gradient):
    first_new = beta_one * first + (1.0 - beta_one) * gradient
    second_new = beta_two * second + (1.0 - beta_two) * gradient * gradient
    corr_one = 1.0 - beta_one**ADAM_STEP
    corr_two = 1.0 - beta_two**ADAM_STEP
    master_new = master - learn_rate * (first_new / corr_one) / (
        jnp.sqrt(second_new / corr_two) + epsilon
    )
    return (master_new, first_new, second_new)


def iota(shape, dim):
    return lax.broadcasted_iota(jnp.int32, shape, dim)


def one_hot(target):
    return jnp.where(iota(target.shape, 1) == target, 1.0, 0.0).astype(BF)


def pick(matrix, values):
    return jnp.dot(matrix, values, preferred_element_type=F32)


def columns(core):
    return pl.ds(pl.multiple_of(core * HALF, HALF), HALF)


def turned(rows):
    return pltpu.roll(rows, 4, axis=0)


def spread_rows(low_ref, middle_ref, second_ref):
    y = lax.axis_index("y")
    return jnp.where(y == 0, low_ref[...], jnp.where(y == 1, middle_ref[...], second_ref[...]))


def pair_kernel(master_ref, first_ref, second_ref, low_ref, middle_ref, pair_ref, rows_ref):
    other = columns(1 - lax.axis_index("core"))
    for i, ref in enumerate((master_ref, first_ref, second_ref)):
        pair_ref[2 * i : 2 * i + 2, :] = ref[:, other]
    rows_ref[...] = spread_rows(low_ref, middle_ref, second_ref)
    pair_ref[6:8, :] = rows_ref[:, other]


def add_kernel(
    own_ref, got_ref, master_ref, first_ref, second_ref, low_ref, middle_ref, pair_ref,
    out_ref, old_ref, rows_ref, split_ref,
):
    core = lax.axis_index("core")
    low = iota((8, 1024), 0) < 4

    def kept(i, carry):
        rows = pl.ds(pl.multiple_of(16 * i, 16), 16)
        parts = []
        for k in range(4):
            cut = slice(k * 1024, (k + 1) * 1024)
            parts.append(own_ref[rows, cut].astype(F32) + got_ref[rows, cut].astype(F32))
        for tile in range(2):
            c = [part[8 * tile : 8 * tile + 8] for part in parts]
            even = [jnp.where(low, c[k], turned(c[k + 1])) for k in (0, 2)]
            odd = [jnp.where(low, turned(c[k]), c[k + 1]) for k in (0, 2)]
            for chip, block in ((4 * i + 2 * tile, even), (4 * i + 2 * tile + 1, odd)):
                out_ref[chip, :, 0:1024] = jnp.concatenate(block, axis=0).astype(BF)
        for chip in range(4):
            out_ref[4 * i + chip, :, 1024:1152] = jnp.zeros((16, 128), BF)
        return carry

    lax.fori_loop(0, 12, kept, 0)

    rows_ref[...] = spread_rows(low_ref, middle_ref, second_ref)
    for mine in range(2):

        @pl.when(core == mine)
        def _():
            for i, ref in enumerate((master_ref, first_ref, second_ref, rows_ref)):
                at = 4 * i + 2 * mine
                old_ref[at : at + 2, :] = ref[:, mine * HALF : (mine + 1) * HALF]
                at = 4 * i + 2 * (1 - mine)
                old_ref[at : at + 2, :] = pair_ref[2 * i : 2 * i + 2, :]

    passed = old_ref[12:16, :]
    high = passed.astype(BF).astype(F32)
    split_ref[0:4, :] = high
    split_ref[4:8, :] = passed - high

    def leave(q, carry):
        cut = pl.ds(pl.multiple_of(q * 256, 256), 256)
        for a in range(4):
            rows = slice(192 + 16 * a, 208 + 16 * a)
            total = own_ref[rows, cut].astype(F32) + got_ref[rows, cut].astype(F32)
            out_ref[48 + q, :, a * 256 : (a + 1) * 256] = total.astype(BF)
        parts = split_ref[:, cut]
        out_ref[48 + q, :, 1024:1152] = jnp.concatenate([parts[:, 0:128], parts[:, 128:256]], axis=0).astype(BF)
        return carry

    lax.fori_loop(0, 16, leave, 0)


def adam_kernel(parts_ref, chip_ref, owner_ref, out_ref, own_ref, other_ref, key_ref, old_ref):
    leaving = lax.axis_index("y") == 3
    core = lax.axis_index("core")

    def add(d, total):
        return total + parts_ref[d, :, 0:1024].astype(F32)

    gradient = lax.fori_loop(1, 64, add, parts_ref[0, :, 0:1024].astype(F32), unroll=7)

    @pl.when(leaving)
    def _():
        for i, y in enumerate((0, 1, 3)):
            for q in range(16):
                parts = parts_ref[16 * y + q, :, 1024:1152].astype(F32)
                for h in range(2):
                    value = parts[8 * h : 8 * h + 4] + parts[8 * h + 4 : 8 * h + 8]
                    at = (q // 4) * 256 + h * 128
                    old_ref[i, 4 * (q % 4) : 4 * (q % 4) + 4, at : at + 128] = value

    @pl.when(jnp.logical_not(leaving))
    def _():
        for i in range(3):
            for k in range(4):
                old_ref[i, 4 * k : 4 * k + 4, :] = chip_ref[4 * i : 4 * i + 4, k * 1024 : (k + 1) * 1024]

    new = adam_update(old_ref[0], old_ref[1], old_ref[2], gradient)
    own_ref[6:8, :] = jnp.zeros((2, HALF), F32)
    other_ref[6:8, :] = jnp.zeros((2, HALF), F32)
    values = [jnp.where(leaving, jnp.zeros_like(value), value) for value in new]
    for mine in range(2):

        @pl.when(core == mine)
        def _():
            for i in range(3):
                for k in range(4):
                    cut = slice(k * 1024, (k + 1) * 1024)
                    at = 4 * k + 2 * mine
                    own_ref[2 * i : 2 * i + 2, cut] = values[i][at : at + 2, :]
                    at = 4 * k + 2 * (1 - mine)
                    other_ref[2 * i : 2 * i + 2, cut] = values[i][at : at + 2, :]

    weights = new[0].astype(BF)

    def spread(d, carry):
        out_ref[d, :, 0:1024] = weights
        return carry

    lax.fori_loop(0, 64, spread, 0, unroll=8)

    lane, row = iota((64, 256), 1), iota((64, 256), 0)
    tiled = jnp.where((lane & 63) == row, 1.0, 0.0).astype(BF)
    across = pick(jnp.broadcast_to(owner_ref[...], (64, 64)).astype(F32).astype(BF), tiled)
    down = jnp.sum(jnp.where(lane == row, across, 0.0), axis=1, keepdims=True)
    earlier = (across == down) & (row < (lane & 63))
    slot = jnp.sum(jnp.where(earlier, 1.0, 0.0), axis=0, keepdims=True)
    key = (across[0:1, :] * 2.0 + slot).astype(jnp.int32) + 512 * (iota((1, 256), 1) >> 6)
    key_ref[...] = key
    moments = jnp.concatenate(
        [
            new[1 + part // 2][:, a * 256 + (part % 2) * 128 : a * 256 + (part % 2) * 128 + 128]
            for part in range(4)
            for a in range(4)
        ],
        axis=0,
    ).astype(BF)
    p = iota((1024, 256), 0)
    wanted = (p >> 4) * 4 + (p & 3) + 512 * ((p >> 2) & 3)
    chosen = jnp.where(key == wanted, 1.0, 0.0).astype(BF)
    out_ref[:, :, 1024:1152] = pick(chosen, moments).astype(BF).reshape(64, 16, 128)


def place_half(blocks_ref, key_ref, weights_ref, adopted_ref, adopted_at, rows_ref, sems, core, side):
    chip = (lax.axis_index("y") * 4 + lax.axis_index("z")) * 4 + lax.axis_index("x")
    low = iota((8, 1024), 0) < 4

    def store(i):
        rows = pl.ds(pl.multiple_of(32 * i, 32), 32)
        return pltpu.make_async_copy(rows_ref.at[rows, :], weights_ref.at[rows, columns(side)], sems.at[i])

    def kept(i, carry):
        for g in range(2):
            tiles = []
            for tile in range(2):
                number = 8 * i + 4 * g + 2 * tile
                even = blocks_ref[number, :, 0:1024].astype(F32)
                odd = blocks_ref[number + 1, :, 0:1024].astype(F32)
                cut = []
                for s in (slice(0, 8), slice(8, 16)):
                    cut.append(jnp.where(low, even[s], turned(odd[s])))
                    cut.append(jnp.where(low, turned(even[s]), odd[s]))
                tiles.append(cut)
            rows = pl.ds(pl.multiple_of(32 * i + 16 * g, 16), 16)
            for k in range(4):
                rows_ref[rows, k * 1024 : (k + 1) * 1024] = jnp.concatenate(
                    [tiles[0][k], tiles[1][k]], axis=0
                ).astype(BF)
        store(i).start()
        return carry

    lax.fori_loop(0, 6, kept, 0)
    for q in range(16):
        for a in range(4):
            rows_ref[192 + 16 * a : 208 + 16 * a, q * 256 : (q + 1) * 256] = blocks_ref[
                48 + q, :, a * 256 : (a + 1) * 256
            ]
    for i in range(6, 8):
        store(i).start()
    k = iota((8, 64), 0)
    wanted = jnp.where(k < 2, chip * 4 + core * 2 + k, -1)
    chosen = jnp.where(key_ref[:, 0:64] == wanted, 1.0, 0.0).astype(BF)
    masters = pick(chosen, rows_ref[192:256, :])
    adopted_ref[0, :, adopted_at(0, HALF)] = masters[0:2, :]
    moments = jnp.concatenate([blocks_ref[48 + q, :, 1024:1152] for q in range(16)], axis=1)
    for h in range(2):
        k = iota((8, 16), 0)
        found = pick(one_hot(jnp.where(k < 4, ((k >> 1) * 2 + h) * 4 + core * 2 + (k & 1), -1)), moments)
        for q in range(16):
            for i in range(2):
                adopted_ref[1 + i, :, adopted_at(q * 256 + h * 128, 128)] = found[
                    2 * i : 2 * i + 2, q * 128 : (q + 1) * 128
                ]
    for i in range(8):
        store(i).wait()


def place_own_kernel(blocks_ref, key_ref, weights_ref, adopted_ref, rows_ref, sems):
    core = lax.axis_index("core")
    place_half(
        blocks_ref, key_ref, weights_ref, adopted_ref, lambda start, size: slice(start, start + size),
        rows_ref, sems, core, core,
    )


def place_other_kernel(
    blocks_ref, key_ref, _, half_ref, own_ref, other_ref, weights_ref, adopted_ref, kept_ref, rows_ref, sems
):
    core = lax.axis_index("core")
    side = 1 - core

    def at(start, size):
        return pl.ds(pl.multiple_of(side * HALF + start, 128), size)

    place_half(blocks_ref, key_ref, weights_ref, adopted_ref, at, rows_ref, sems, core, side)
    for i in range(3):
        adopted_ref[i, :, columns(core)] = half_ref[i]
        kept_ref[i, :, columns(core)] = own_ref[2 * i : 2 * i + 2, :]
        kept_ref[i, :, columns(side)] = other_ref[2 * i : 2 * i + 2, :]


def params(mib=40):
    return pltpu.CompilerParams(vmem_limit_bytes=mib * 1024 * 1024)


def shape(dims, dtype):
    return jax.ShapeDtypeStruct(dims, dtype)


def swapped(value):
    return lax.ppermute(value, "core", [(0, 1), (1, 0)])


def from_leaving(value, group):
    return lax.ppermute(value, ("y", "z", "x", "core"), [(96 + rank, 32 * group + rank) for rank in range(32)])


def body(local_grads, master, first, second, new_owner):
    grads = local_grads.reshape(256, 8192)
    vmem = pl.BlockSpec(memory_space=pltpu.VMEM)
    hbm = pl.BlockSpec(memory_space=pltpu.HBM)
    core = lax.axis_index("core")
    got = swapped(lax.dynamic_slice(grads, (0, (1 - core) * HALF), (256, HALF)))
    own = lax.dynamic_slice(grads, (0, core * HALF), (256, HALF))
    low, middle = from_leaving(master, 0), from_leaving(first, 1)
    pair = pl.pallas_call(
        pair_kernel,
        in_specs=[vmem] * 5,
        out_specs=vmem,
        out_shape=shape((8, HALF), F32),
        scratch_shapes=[pltpu.VMEM((2, 8192), F32)],
        compiler_params=params(),
        name="pair",
    )(master, first, second, low, middle)
    pair = swapped(pair)
    partial, old = pl.pallas_call(
        add_kernel,
        in_specs=[vmem] * 8,
        out_specs=[vmem] * 2,
        out_shape=[shape((64, 16, 1152), BF), shape((16, HALF), F32)],
        scratch_shapes=[pltpu.VMEM((2, 8192), F32), pltpu.VMEM((8, HALF), F32)],
        compiler_params=params(),
        name="add_blocks",
    )(own, got, master, first, second, low, middle, pair)
    partial = lax.all_to_all(partial, CHIPS, 0, 0, tiled=True)
    payload, own_new, other_new, key = pl.pallas_call(
        adam_kernel,
        in_specs=[vmem] * 3,
        out_specs=[vmem] * 4,
        out_shape=[
            shape((64, 16, 1152), BF),
            shape((8, HALF), F32),
            shape((8, HALF), F32),
            shape((1, 256), jnp.int32),
        ],
        scratch_shapes=[pltpu.VMEM((3, 16, 1024), F32)],
        compiler_params=params(),
        name="adam",
    )(partial, old, new_owner.reshape(1, 64))
    other_new = swapped(other_new)
    blocks = lax.all_to_all(payload, CHIPS, 0, 0, tiled=True)
    other_blocks = swapped(blocks)
    scratch = [pltpu.VMEM((256, HALF), BF), pltpu.SemaphoreType.DMA((8,))]
    weights, adopted = pl.pallas_call(
        place_own_kernel,
        in_specs=[vmem, vmem],
        out_specs=[hbm, vmem],
        out_shape=[shape((256, 8192), BF), shape((3, 2, HALF), F32)],
        scratch_shapes=scratch,
        compiler_params=params(),
        cost_estimate=pl.CostEstimate(flops=8_000_000, bytes_accessed=8_000_000, transcendentals=0),
        name="place_own",
    )(blocks, key)
    weights, adopted, kept = pl.pallas_call(
        place_other_kernel,
        in_specs=[vmem, vmem, hbm, vmem, vmem, vmem],
        out_specs=[hbm, vmem, vmem],
        out_shape=[shape((256, 8192), BF), shape((3, 2, 8192), F32), shape((3, 2, 8192), F32)],
        scratch_shapes=scratch,
        input_output_aliases={2: 0},
        compiler_params=params(),
        name="place_other",
    )(other_blocks, key, weights, adopted, own_new, other_new)
    return (weights, kept.transpose(1, 0, 2), adopted.transpose(1, 0, 2)[None, None])


def solution(mesh):
    fine = Mesh(mesh.devices.reshape(4, 4, 4, 2), ("y", "z", "x", "core"))
    every = ("y", "z", "x", "core")
    in_specs = (P("y", ("z", "x", "core"), None, None), P(every, None), P(every, None), P(every, None), P())
    out_specs = (P(), P(every, None, None), P("y", ("z", "x", "core"), None, None, None))
    return jax.shard_map(body, mesh=fine, in_specs=in_specs, out_specs=out_specs, check_vma=False)
```

```python
import jax
import jax.numpy as jnp
from jax import lax
from jax.experimental import pallas as pl
from jax.experimental.pallas import tpu as pltpu
from jax.sharding import Mesh
from jax.sharding import PartitionSpec as P

ADAM_STEP = 20

beta_one = 0.9
beta_two = 0.95
learn_rate = 0.05
epsilon = 1e-08

CHIPS = ("y", "z", "x")
BF = jnp.bfloat16
F32 = jnp.float32
HALF = 4096


def adam_update(master, first, second, gradient):
    first_new = beta_one * first + (1.0 - beta_one) * gradient
    second_new = beta_two * second + (1.0 - beta_two) * gradient * gradient
    corr_one = 1.0 - beta_one**ADAM_STEP
    corr_two = 1.0 - beta_two**ADAM_STEP
    master_new = master - learn_rate * (first_new / corr_one) / (
        jnp.sqrt(second_new / corr_two) + epsilon
    )
    return (master_new, first_new, second_new)


def iota(shape, dim):
    return lax.broadcasted_iota(jnp.int32, shape, dim)


def one_hot(target):
    return jnp.where(iota(target.shape, 1) == target, 1.0, 0.0).astype(BF)


def pick(matrix, values):
    return jnp.dot(matrix, values, preferred_element_type=F32)


def columns(core):
    return pl.ds(pl.multiple_of(core * HALF, HALF), HALF)


def turned(rows):
    return pltpu.roll(rows, 4, axis=0)


def spread_rows(low_ref, middle_ref, second_ref):
    y = lax.axis_index("y")
    return jnp.where(y == 0, low_ref[...], jnp.where(y == 1, middle_ref[...], second_ref[...]))


def chip_class(chip):
    return (chip & 1) ^ (((chip >> 4) & 1) * 2) ^ (((chip >> 2) & 1) * 3)


def own_chip():
    return (lax.axis_index("y") * 4 + lax.axis_index("z")) * 4 + lax.axis_index("x")


def quarter(number):
    return pl.ds(pl.multiple_of(number * 256, 256), 256)


def add_kernel(
    own_ref, got_ref, master_ref, first_ref, second_ref, low_ref, middle_ref,
    keep_ref, x_up, x_down, y_up, y_down, z_up, z_down, pair_ref, blocks_ref, rows_ref,
):
    other = columns(1 - lax.axis_index("core"))
    for i, ref in enumerate((master_ref, first_ref, second_ref)):
        pair_ref[2 * i : 2 * i + 2, :] = ref[:, other]
    rows_ref[...] = spread_rows(low_ref, middle_ref, second_ref)
    pair_ref[6:8, :] = rows_ref[:, other]
    low = iota((8, 1024), 0) < 4

    def kept(i, carry):
        rows = pl.ds(pl.multiple_of(16 * i, 16), 16)
        parts = []
        for k in range(4):
            cut = slice(k * 1024, (k + 1) * 1024)
            parts.append(own_ref[rows, cut].astype(F32) + got_ref[rows, cut].astype(F32))
        for tile in range(2):
            c = [part[8 * tile : 8 * tile + 8] for part in parts]
            even = [jnp.where(low, c[k], turned(c[k + 1])) for k in (0, 2)]
            odd = [jnp.where(low, turned(c[k]), c[k + 1]) for k in (0, 2)]
            for chip, block in ((4 * i + 2 * tile, even), (4 * i + 2 * tile + 1, odd)):
                blocks_ref[chip] = jnp.concatenate(block, axis=0).astype(BF)
        return carry

    lax.fori_loop(0, 12, kept, 0)

    def leave(q, carry):
        cut = pl.ds(pl.multiple_of(q * 256, 256), 256)
        for a in range(4):
            rows = slice(192 + 16 * a, 208 + 16 * a)
            total = own_ref[rows, cut].astype(F32) + got_ref[rows, cut].astype(F32)
            blocks_ref[48 + q, :, a * 256 : (a + 1) * 256] = total.astype(BF)
        return carry

    lax.fori_loop(0, 16, leave, 0)
    kind = chip_class(own_chip())
    keep_ref[...] = blocks_ref[:, :, quarter(kind)]
    for axis, (up, down) in enumerate(((x_up, x_down), (y_up, y_down), (z_up, z_down))):
        up[...] = blocks_ref[0:32, :, quarter(kind ^ (axis + 1))]
        down[...] = blocks_ref[32:64, :, quarter(kind ^ (axis + 1))]


def merge_kernel(
    keep_ref, x_up, x_down, y_up, y_down, z_up, z_down,
    master_ref, first_ref, second_ref, low_ref, middle_ref, pair_ref,
    out_ref, old_ref, rows_ref, split_ref,
):
    core = lax.axis_index("core")

    def add(d, carry):
        for base, refs in ((0, (x_up, y_up, z_up)), (32, (x_down, y_down, z_down))):
            total = keep_ref[base + d].astype(F32)
            for ref in refs:
                total = total + ref[d].astype(F32)
            out_ref[base + d, :, 0:256] = total.astype(BF)
        return carry

    lax.fori_loop(0, 32, add, 0, unroll=8)

    rows_ref[...] = spread_rows(low_ref, middle_ref, second_ref)
    for mine in range(2):

        @pl.when(core == mine)
        def _():
            for i, ref in enumerate((master_ref, first_ref, second_ref, rows_ref)):
                at = 4 * i + 2 * mine
                old_ref[at : at + 2, :] = ref[:, mine * HALF : (mine + 1) * HALF]
                at = 4 * i + 2 * (1 - mine)
                old_ref[at : at + 2, :] = pair_ref[2 * i : 2 * i + 2, :]

    passed = old_ref[12:16, :]
    high = passed.astype(BF).astype(F32)
    split_ref[0:4, :] = high
    split_ref[4:8, :] = passed - high

    def empty(d, carry):
        out_ref[d, :, 256:384] = jnp.zeros((16, 128), BF)
        return carry

    lax.fori_loop(0, 48, empty, 0, unroll=8)

    def leave(q, carry):
        parts = split_ref[:, quarter(q)]
        out_ref[48 + q, :, 256:384] = jnp.concatenate([parts[:, 0:128], parts[:, 128:256]], axis=0).astype(BF)
        return carry

    lax.fori_loop(0, 16, leave, 0, unroll=4)


def adam_kernel(parts_ref, chip_ref, owner_ref, out_ref, own_ref, other_ref, key_ref, old_ref):
    leaving = lax.axis_index("y") == 3
    core = lax.axis_index("core")
    totals = [jnp.zeros((16, 256), F32)] * 4
    for chip in range(64):
        kind = chip_class(chip)
        totals[kind] = totals[kind] + parts_ref[chip, :, 0:256].astype(F32)
    gradient = jnp.concatenate(totals, axis=1)

    @pl.when(leaving)
    def _():
        for i, y in enumerate((0, 1, 3)):
            for q in range(16):
                parts = parts_ref[16 * y + q, :, 256:384].astype(F32)
                for h in range(2):
                    value = parts[8 * h : 8 * h + 4] + parts[8 * h + 4 : 8 * h + 8]
                    at = (q // 4) * 256 + h * 128
                    old_ref[i, 4 * (q % 4) : 4 * (q % 4) + 4, at : at + 128] = value

    @pl.when(jnp.logical_not(leaving))
    def _():
        for i in range(3):
            for k in range(4):
                old_ref[i, 4 * k : 4 * k + 4, :] = chip_ref[4 * i : 4 * i + 4, k * 1024 : (k + 1) * 1024]

    new = adam_update(old_ref[0], old_ref[1], old_ref[2], gradient)
    own_ref[6:8, :] = jnp.zeros((2, HALF), F32)
    other_ref[6:8, :] = jnp.zeros((2, HALF), F32)
    values = [jnp.where(leaving, jnp.zeros_like(value), value) for value in new]
    for mine in range(2):

        @pl.when(core == mine)
        def _():
            for i in range(3):
                for k in range(4):
                    cut = slice(k * 1024, (k + 1) * 1024)
                    at = 4 * k + 2 * mine
                    own_ref[2 * i : 2 * i + 2, cut] = values[i][at : at + 2, :]
                    at = 4 * k + 2 * (1 - mine)
                    other_ref[2 * i : 2 * i + 2, cut] = values[i][at : at + 2, :]

    weights = new[0].astype(BF)

    for chip in range(64):
        kind = chip_class(chip)
        out_ref[chip, :, 0:256] = weights[:, kind * 256 : (kind + 1) * 256]

    lane, row = iota((64, 256), 1), iota((64, 256), 0)
    tiled = jnp.where((lane & 63) == row, 1.0, 0.0).astype(BF)
    across = pick(jnp.broadcast_to(owner_ref[...], (64, 64)).astype(F32).astype(BF), tiled)
    down = jnp.sum(jnp.where(lane == row, across, 0.0), axis=1, keepdims=True)
    earlier = (across == down) & (row < (lane & 63))
    slot = jnp.sum(jnp.where(earlier, 1.0, 0.0), axis=0, keepdims=True)
    key = (across[0:1, :] * 2.0 + slot).astype(jnp.int32) + 512 * (iota((1, 256), 1) >> 6)
    key_ref[...] = key
    moments = jnp.concatenate(
        [
            new[1 + part // 2][:, a * 256 + (part % 2) * 128 : a * 256 + (part % 2) * 128 + 128]
            for part in range(4)
            for a in range(4)
        ],
        axis=0,
    ).astype(BF)
    p = iota((1024, 256), 0)
    wanted = (p >> 4) * 4 + (p & 3) + 512 * ((p >> 2) & 3)
    chosen = jnp.where(key == wanted, 1.0, 0.0).astype(BF)
    out_ref[:, :, 256:384] = pick(chosen, moments).astype(BF).reshape(64, 16, 128)


def halve_kernel(blocks_ref, *out_refs):
    for i, ref in enumerate(out_refs):
        ref[...] = blocks_ref[32 * (i % 2) : 32 * (i % 2) + 32, :, 0:256]


def join_kernel(blocks_ref, x_up, x_down, y_up, y_down, z_up, z_down, out_ref):
    out_ref[:, :, 0:384] = blocks_ref[...]
    for at, up, down in ((384, x_up, x_down), (640, y_up, y_down), (896, z_up, z_down)):
        out_ref[0:32, :, at : at + 256] = up[...]
        out_ref[32:64, :, at : at + 256] = down[...]


def place_half(views, key_ref, weights_ref, adopted_ref, adopted_at, rows_ref, sems, core, side):
    blocks_ref = views[0][0][0]
    chip = own_chip()
    kind = chip_class(chip)
    low = iota((8, 256), 0) < 4

    def store(i):
        rows = pl.ds(pl.multiple_of(32 * i, 32), 32)
        return pltpu.make_async_copy(rows_ref.at[rows, :], weights_ref.at[rows, columns(side)], sems.at[i])

    def kept(last, i, carry):
        for axis in range(4):
            ref, base, lane = views[axis][last]
            for g in range(2):
                tiles = []
                for tile in range(2):
                    number = 8 * i + 4 * g + 2 * tile - base
                    even = ref[number, :, lane : lane + 256].astype(F32)
                    odd = ref[number + 1, :, lane : lane + 256].astype(F32)
                    cut = []
                    for s in (slice(0, 8), slice(8, 16)):
                        cut.append(jnp.where(low, even[s], turned(odd[s])))
                        cut.append(jnp.where(low, turned(even[s]), odd[s]))
                    tiles.append(cut)
                rows = pl.ds(pl.multiple_of(32 * i + 16 * g, 16), 16)
                for k in range(4):
                    rows_ref[rows, quarter((kind ^ axis) + 4 * k)] = jnp.concatenate(
                        [tiles[0][k], tiles[1][k]], axis=0
                    ).astype(BF)
        store(i).start()
        return carry

    lax.fori_loop(0, 4, lambda i, carry: kept(0, i, carry), 0)
    lax.fori_loop(4, 6, lambda i, carry: kept(1, i, carry), 0)
    for axis in range(4):
        ref, base, lane = views[axis][1]
        rows = pl.ds(pl.multiple_of(192 + 16 * (kind ^ axis), 16), 16)
        for q in range(16):
            rows_ref[rows, q * 256 : (q + 1) * 256] = ref[48 + q - base, :, lane : lane + 256]
    for i in range(6, 8):
        store(i).start()
    k = iota((8, 64), 0)
    wanted = jnp.where(k < 2, chip * 4 + core * 2 + k, -1)
    chosen = jnp.where(key_ref[:, 0:64] == wanted, 1.0, 0.0).astype(BF)
    masters = pick(chosen, rows_ref[192:256, :])
    adopted_ref[0, :, adopted_at(0, HALF)] = masters[0:2, :]
    moments = jnp.concatenate([blocks_ref[48 + q, :, 256:384] for q in range(16)], axis=1)
    for h in range(2):
        k = iota((8, 16), 0)
        found = pick(one_hot(jnp.where(k < 4, ((k >> 1) * 2 + h) * 4 + core * 2 + (k & 1), -1)), moments)
        for q in range(16):
            for i in range(2):
                adopted_ref[1 + i, :, adopted_at(q * 256 + h * 128, 128)] = found[
                    2 * i : 2 * i + 2, q * 128 : (q + 1) * 128
                ]
    for i in range(8):
        store(i).wait()


def place_own_kernel(*refs):
    blocks_ref, *pieces = refs[:7]
    key_ref, weights_ref, adopted_ref, rows_ref, sems = refs[7:]
    views = [[(blocks_ref, 0, 0)] * 2]
    views += [[(pieces[2 * axis + last], 32 * last, 0) for last in range(2)] for axis in range(3)]
    core = lax.axis_index("core")
    place_half(
        views, key_ref, weights_ref, adopted_ref, lambda start, size: slice(start, start + size),
        rows_ref, sems, core, core,
    )


def place_other_kernel(*refs):
    joined_ref, key_ref, _, half_ref, own_ref, other_ref = refs[:6]
    weights_ref, adopted_ref, kept_ref, rows_ref, sems = refs[6:]
    views = [[(joined_ref, 0, lane)] * 2 for lane in (0, 384, 640, 896)]
    core = lax.axis_index("core")
    side = 1 - core

    def at(start, size):
        return pl.ds(pl.multiple_of(side * HALF + start, 128), size)

    place_half(views, key_ref, weights_ref, adopted_ref, at, rows_ref, sems, core, side)
    for i in range(3):
        adopted_ref[i, :, columns(core)] = half_ref[i]
        kept_ref[i, :, columns(core)] = own_ref[2 * i : 2 * i + 2, :]
        kept_ref[i, :, columns(side)] = other_ref[2 * i : 2 * i + 2, :]


def params(mib=40):
    return pltpu.CompilerParams(vmem_limit_bytes=mib * 1024 * 1024)


def shape(dims, dtype):
    return jax.ShapeDtypeStruct(dims, dtype)


def swapped(value):
    return lax.ppermute(value, "core", [(0, 1), (1, 0)])


def to_neighbours(up_and_down):
    got = []
    for i, axis in enumerate(("x", "y", "z")):
        for value, shift in zip(up_and_down[2 * i : 2 * i + 2], (1, 3)):
            got.append(lax.ppermute(value, axis, [(p, (p + shift) % 4) for p in range(4)]))
    return got


def from_leaving(value, group):
    return lax.ppermute(value, ("y", "z", "x", "core"), [(96 + rank, 32 * group + rank) for rank in range(32)])


def body(local_grads, master, first, second, new_owner):
    grads = local_grads.reshape(256, 8192)
    vmem = pl.BlockSpec(memory_space=pltpu.VMEM)
    hbm = pl.BlockSpec(memory_space=pltpu.HBM)
    core = lax.axis_index("core")
    got = swapped(lax.dynamic_slice(grads, (0, (1 - core) * HALF), (256, HALF)))
    own = lax.dynamic_slice(grads, (0, core * HALF), (256, HALF))
    low, middle = from_leaving(master, 0), from_leaving(first, 1)
    piece = shape((32, 16, 256), BF)
    *to_send, pair = pl.pallas_call(
        add_kernel,
        in_specs=[vmem] * 7,
        out_specs=[vmem] * 8,
        out_shape=[shape((64, 16, 256), BF)] + [piece] * 6 + [shape((8, HALF), F32)],
        scratch_shapes=[pltpu.VMEM((64, 16, 1024), BF), pltpu.VMEM((2, 8192), F32)],
        compiler_params=params(),
        name="add_blocks",
    )(own, got, master, first, second, low, middle)
    keep, *to_send = to_send
    arrived = to_neighbours(to_send)
    pair = swapped(pair)
    partial, old = pl.pallas_call(
        merge_kernel,
        in_specs=[vmem] * 13,
        out_specs=[vmem] * 2,
        out_shape=[shape((64, 16, 384), BF), shape((16, HALF), F32)],
        scratch_shapes=[pltpu.VMEM((2, 8192), F32), pltpu.VMEM((8, HALF), F32)],
        compiler_params=params(),
        name="merge",
    )(keep, *arrived, master, first, second, low, middle, pair)
    partial = lax.all_to_all(partial, CHIPS, 0, 0, tiled=True)
    payload, own_new, other_new, key = pl.pallas_call(
        adam_kernel,
        in_specs=[vmem] * 3,
        out_specs=[vmem] * 4,
        out_shape=[
            shape((64, 16, 384), BF),
            shape((8, HALF), F32),
            shape((8, HALF), F32),
            shape((1, 256), jnp.int32),
        ],
        scratch_shapes=[pltpu.VMEM((3, 16, 1024), F32)],
        compiler_params=params(),
        name="adam",
    )(partial, old, new_owner.reshape(1, 64))
    other_new = swapped(other_new)
    blocks = lax.all_to_all(payload, CHIPS, 0, 0, tiled=True)
    halves = pl.pallas_call(
        halve_kernel,
        in_specs=[vmem],
        out_specs=[vmem] * 6,
        out_shape=[piece] * 6,
        compiler_params=params(),
        name="halve",
    )(blocks)
    pieces = [blocks] + to_neighbours(halves)
    joined = pl.pallas_call(
        join_kernel,
        in_specs=[vmem] * 7,
        out_specs=vmem,
        out_shape=shape((64, 16, 1152), BF),
        compiler_params=params(),
        name="join",
    )(*pieces)
    other_joined = swapped(joined)
    scratch = [pltpu.VMEM((256, HALF), BF), pltpu.SemaphoreType.DMA((8,))]
    weights, adopted = pl.pallas_call(
        place_own_kernel,
        in_specs=[vmem] * 8,
        out_specs=[hbm, vmem],
        out_shape=[shape((256, 8192), BF), shape((3, 2, HALF), F32)],
        scratch_shapes=scratch,
        compiler_params=params(),
        cost_estimate=pl.CostEstimate(flops=8_000_000, bytes_accessed=8_000_000, transcendentals=0),
        name="place_own",
    )(*pieces, key)
    weights, adopted, kept = pl.pallas_call(
        place_other_kernel,
        in_specs=[vmem] * 2 + [hbm] + [vmem] * 3,
        out_specs=[hbm, vmem, vmem],
        out_shape=[shape((256, 8192), BF), shape((3, 2, 8192), F32), shape((3, 2, 8192), F32)],
        scratch_shapes=scratch,
        input_output_aliases={2: 0},
        compiler_params=params(),
        name="place_other",
    )(other_joined, key, weights, adopted, own_new, other_new)
    return (weights, kept.transpose(1, 0, 2), adopted.transpose(1, 0, 2)[None, None])


def solution(mesh):
    fine = Mesh(mesh.devices.reshape(4, 4, 4, 2), ("y", "z", "x", "core"))
    every = ("y", "z", "x", "core")
    in_specs = (P("y", ("z", "x", "core"), None, None), P(every, None), P(every, None), P(every, None), P())
    out_specs = (P(), P(every, None, None), P("y", ("z", "x", "core"), None, None, None))
    return jax.shard_map(body, mesh=fine, in_specs=in_specs, out_specs=out_specs, check_vma=False)
```

```python
import jax
import jax.numpy as jnp
from jax import lax
from jax.experimental import pallas as pl
from jax.experimental.pallas import tpu as pltpu
from jax.sharding import Mesh
from jax.sharding import PartitionSpec as P

ADAM_STEP = 20

beta_one = 0.9
beta_two = 0.95
learn_rate = 0.05
epsilon = 1e-08

CHIPS = ("y", "z", "x")
BF = jnp.bfloat16
F32 = jnp.float32
HALF = 4096


def adam_update(master, first, second, gradient):
    first_new = beta_one * first + (1.0 - beta_one) * gradient
    second_new = beta_two * second + (1.0 - beta_two) * gradient * gradient
    corr_one = 1.0 - beta_one**ADAM_STEP
    corr_two = 1.0 - beta_two**ADAM_STEP
    master_new = master - learn_rate * (first_new / corr_one) / (
        jnp.sqrt(second_new / corr_two) + epsilon
    )
    return (master_new, first_new, second_new)


def iota(shape, dim):
    return lax.broadcasted_iota(jnp.int32, shape, dim)


def one_hot(target):
    return jnp.where(iota(target.shape, 1) == target, 1.0, 0.0).astype(BF)


def pick(matrix, values):
    return jnp.dot(matrix, values, preferred_element_type=F32)


def columns(core):
    return pl.ds(pl.multiple_of(core * HALF, HALF), HALF)


def turned(rows):
    return pltpu.roll(rows, 4, axis=0)


def spread_rows(low_ref, middle_ref, second_ref):
    y = lax.axis_index("y")
    return jnp.where(y == 0, low_ref[...], jnp.where(y == 1, middle_ref[...], second_ref[...]))


def pair_kernel(master_ref, first_ref, second_ref, low_ref, middle_ref, pair_ref, rows_ref):
    other = columns(1 - lax.axis_index("core"))
    for i, ref in enumerate((master_ref, first_ref, second_ref)):
        pair_ref[2 * i : 2 * i + 2, :] = ref[:, other]
    rows_ref[...] = spread_rows(low_ref, middle_ref, second_ref)
    pair_ref[6:8, :] = rows_ref[:, other]


def chip_class(chip):
    return (chip & 1) ^ (((chip >> 4) & 1) * 2) ^ (((chip >> 2) & 1) * 3)


def own_chip():
    return (lax.axis_index("y") * 4 + lax.axis_index("z")) * 4 + lax.axis_index("x")


def quarter(number):
    return pl.ds(pl.multiple_of(number * 256, 256), 256)


def add_kernel(
    grads_ref, got_ref, low_ref, middle_ref, keep_ref, x_ref, y_ref, z_ref, blocks_ref
):
    core = lax.axis_index("core")
    low = iota((8, 1024), 0) < 4

    def kept(i, carry):
        rows = pl.ds(pl.multiple_of(16 * i, 16), 16)
        parts = []
        for k in range(4):
            cut = pl.ds(pl.multiple_of(core * HALF + k * 1024, 1024), 1024)
            got = got_ref[rows, k * 1024 : (k + 1) * 1024]
            parts.append(grads_ref[rows, cut].astype(F32) + got.astype(F32))
        for tile in range(2):
            c = [part[8 * tile : 8 * tile + 8] for part in parts]
            even = [jnp.where(low, c[k], turned(c[k + 1])) for k in (0, 2)]
            odd = [jnp.where(low, turned(c[k]), c[k + 1]) for k in (0, 2)]
            for chip, block in ((4 * i + 2 * tile, even), (4 * i + 2 * tile + 1, odd)):
                blocks_ref[chip] = jnp.concatenate(block, axis=0).astype(BF)
        return carry

    lax.fori_loop(0, 12, kept, 0)

    def leave(q, carry):
        cut = pl.ds(pl.multiple_of(q * 256, 256), 256)
        own_cut = pl.ds(pl.multiple_of(core * HALF + q * 256, 256), 256)
        for a in range(4):
            rows = slice(192 + 16 * a, 208 + 16 * a)
            total = grads_ref[rows, own_cut].astype(F32) + got_ref[rows, cut].astype(F32)
            blocks_ref[48 + q, :, a * 256 : (a + 1) * 256] = total.astype(BF)
        return carry

    lax.fori_loop(0, 16, leave, 0)
    kind = chip_class(own_chip())
    keep_ref[...] = blocks_ref[:, :, quarter(kind)]
    for axis, ref in enumerate((x_ref, y_ref, z_ref)):
        ref[...] = blocks_ref[:, :, quarter(kind ^ (axis + 1))]


def merge_kernel(
    keep_ref, x_ref, y_ref, z_ref,
    master_ref, first_ref, second_ref, low_ref, middle_ref, pair_ref,
    out_ref, old_ref, rows_ref, split_ref,
):
    core = lax.axis_index("core")

    def add(d, carry):
        total = keep_ref[d].astype(F32)
        for ref in (x_ref, y_ref, z_ref):
            total = total + ref[d].astype(F32)
        out_ref[d, :, 0:256] = total.astype(BF)
        return carry

    lax.fori_loop(0, 64, add, 0, unroll=8)

    rows_ref[...] = spread_rows(low_ref, middle_ref, second_ref)
    for mine in range(2):

        @pl.when(core == mine)
        def _():
            for i, ref in enumerate((master_ref, first_ref, second_ref, rows_ref)):
                at = 4 * i + 2 * mine
                old_ref[at : at + 2, :] = ref[:, mine * HALF : (mine + 1) * HALF]
                at = 4 * i + 2 * (1 - mine)
                old_ref[at : at + 2, :] = pair_ref[2 * i : 2 * i + 2, :]

    passed = old_ref[12:16, :]
    high = passed.astype(BF).astype(F32)
    split_ref[0:4, :] = high
    split_ref[4:8, :] = passed - high

    def empty(d, carry):
        out_ref[d, :, 256:384] = jnp.zeros((16, 128), BF)
        return carry

    lax.fori_loop(0, 48, empty, 0, unroll=8)

    def leave(q, carry):
        parts = split_ref[:, quarter(q)]
        out_ref[48 + q, :, 256:384] = jnp.concatenate([parts[:, 0:128], parts[:, 128:256]], axis=0).astype(BF)
        return carry

    lax.fori_loop(0, 16, leave, 0, unroll=4)


def adam_kernel(parts_ref, chip_ref, owner_ref, out_ref, own_ref, other_ref, key_ref, old_ref):
    leaving = lax.axis_index("y") == 3
    core = lax.axis_index("core")
    totals = [jnp.zeros((16, 256), F32)] * 4
    for chip in range(64):
        kind = chip_class(chip)
        totals[kind] = totals[kind] + parts_ref[chip, :, 0:256].astype(F32)
    gradient = jnp.concatenate(totals, axis=1)

    @pl.when(leaving)
    def _():
        for i, y in enumerate((0, 1, 3)):
            for q in range(16):
                parts = parts_ref[16 * y + q, :, 256:384].astype(F32)
                for h in range(2):
                    value = parts[8 * h : 8 * h + 4] + parts[8 * h + 4 : 8 * h + 8]
                    at = (q // 4) * 256 + h * 128
                    old_ref[i, 4 * (q % 4) : 4 * (q % 4) + 4, at : at + 128] = value

    @pl.when(jnp.logical_not(leaving))
    def _():
        for i in range(3):
            for k in range(4):
                old_ref[i, 4 * k : 4 * k + 4, :] = chip_ref[4 * i : 4 * i + 4, k * 1024 : (k + 1) * 1024]

    new = adam_update(old_ref[0], old_ref[1], old_ref[2], gradient)
    own_ref[6:8, :] = jnp.zeros((2, HALF), F32)
    other_ref[6:8, :] = jnp.zeros((2, HALF), F32)
    values = [jnp.where(leaving, jnp.zeros_like(value), value) for value in new]
    for mine in range(2):

        @pl.when(core == mine)
        def _():
            for i in range(3):
                for k in range(4):
                    cut = slice(k * 1024, (k + 1) * 1024)
                    at = 4 * k + 2 * mine
                    own_ref[2 * i : 2 * i + 2, cut] = values[i][at : at + 2, :]
                    at = 4 * k + 2 * (1 - mine)
                    other_ref[2 * i : 2 * i + 2, cut] = values[i][at : at + 2, :]

    weights = new[0].astype(BF)

    for chip in range(64):
        kind = chip_class(chip)
        out_ref[chip, :, 0:256] = weights[:, kind * 256 : (kind + 1) * 256]

    lane, row = iota((64, 256), 1), iota((64, 256), 0)
    tiled = jnp.where((lane & 63) == row, 1.0, 0.0).astype(BF)
    across = pick(jnp.broadcast_to(owner_ref[...], (64, 64)).astype(F32).astype(BF), tiled)
    down = jnp.sum(jnp.where(lane == row, across, 0.0), axis=1, keepdims=True)
    earlier = (across == down) & (row < (lane & 63))
    slot = jnp.sum(jnp.where(earlier, 1.0, 0.0), axis=0, keepdims=True)
    key = (across[0:1, :] * 2.0 + slot).astype(jnp.int32) + 512 * (iota((1, 256), 1) >> 6)
    key_ref[...] = key
    moments = jnp.concatenate(
        [
            new[1 + part // 2][:, a * 256 + (part % 2) * 128 : a * 256 + (part % 2) * 128 + 128]
            for part in range(4)
            for a in range(4)
        ],
        axis=0,
    ).astype(BF)
    p = iota((1024, 256), 0)
    wanted = (p >> 4) * 4 + (p & 3) + 512 * ((p >> 2) & 3)
    chosen = jnp.where(key == wanted, 1.0, 0.0).astype(BF)
    out_ref[:, :, 256:384] = pick(chosen, moments).astype(BF).reshape(64, 16, 128)


def copy_kernel(blocks_ref, out_ref):
    out_ref[...] = blocks_ref[:, :, 0:256]


def join_kernel(blocks_ref, x_ref, y_ref, z_ref, out_ref):
    out_ref[:, :, 0:384] = blocks_ref[...]
    for at, ref in ((384, x_ref), (640, y_ref), (896, z_ref)):
        out_ref[:, :, at : at + 256] = ref[...]


def place_half(views, key_ref, weights_ref, adopted_ref, adopted_at, adopted_ready, rows_ref, sems, core, side):
    blocks_ref = views[0][0]
    chip = own_chip()
    kind = chip_class(chip)
    low = iota((8, 256), 0) < 4

    def store(i):
        rows = pl.ds(pl.multiple_of(32 * i, 32), 32)
        return pltpu.make_async_copy(rows_ref.at[rows, :], weights_ref.at[rows, columns(side)], sems.at[i])

    def kept(i, carry):
        for axis in range(4):
            ref, lane = views[axis]
            for g in range(2):
                tiles = []
                for tile in range(2):
                    number = 8 * i + 4 * g + 2 * tile
                    even = ref[number, :, lane : lane + 256].astype(F32)
                    odd = ref[number + 1, :, lane : lane + 256].astype(F32)
                    cut = []
                    for s in (slice(0, 8), slice(8, 16)):
                        cut.append(jnp.where(low, even[s], turned(odd[s])))
                        cut.append(jnp.where(low, turned(even[s]), odd[s]))
                    tiles.append(cut)
                rows = pl.ds(pl.multiple_of(32 * i + 16 * g, 16), 16)
                for k in range(4):
                    rows_ref[rows, quarter((kind ^ axis) + 4 * k)] = jnp.concatenate(
                        [tiles[0][k], tiles[1][k]], axis=0
                    ).astype(BF)
        store(i).start()
        return carry

    for axis in range(4):
        ref, lane = views[axis]
        rows = pl.ds(pl.multiple_of(192 + 16 * (kind ^ axis), 16), 16)
        for q in range(16):
            rows_ref[rows, q * 256 : (q + 1) * 256] = ref[48 + q, :, lane : lane + 256]
    for i in range(6, 8):
        store(i).start()
    k = iota((8, 64), 0)
    wanted = jnp.where(k < 2, chip * 4 + core * 2 + k, -1)
    chosen = jnp.where(key_ref[:, 0:64] == wanted, 1.0, 0.0).astype(BF)
    masters = pick(chosen, rows_ref[192:256, :])
    adopted_ref[0, :, adopted_at(0, HALF)] = masters[0:2, :]
    moments = jnp.concatenate([blocks_ref[48 + q, :, 256:384] for q in range(16)], axis=1)
    for h in range(2):
        k = iota((8, 16), 0)
        found = pick(one_hot(jnp.where(k < 4, ((k >> 1) * 2 + h) * 4 + core * 2 + (k & 1), -1)), moments)
        for q in range(16):
            for i in range(2):
                adopted_ref[1 + i, :, adopted_at(q * 256 + h * 128, 128)] = found[
                    2 * i : 2 * i + 2, q * 128 : (q + 1) * 128
                ]
    adopted_ready()
    lax.fori_loop(0, 6, kept, 0)
    for i in range(8):
        store(i).wait()


def place_own_kernel(
    blocks_ref, x_ref, y_ref, z_ref, key_ref, weights_ref, adopted_ref, rows_ref, sems
):
    views = [(ref, 0) for ref in (blocks_ref, x_ref, y_ref, z_ref)]
    core = lax.axis_index("core")
    place_half(
        views, key_ref, weights_ref, adopted_ref, lambda start, size: slice(start, start + size), lambda: None,
        rows_ref, sems, core, core,
    )


def place_other_kernel(*refs):
    joined_ref, key_ref, _, half_ref, own_ref, other_ref = refs[:6]
    weights_ref, adopted_out, kept_out, adopted_ref, kept_ref, rows_ref, sems, out_sems = refs[6:]
    views = [(joined_ref, lane) for lane in (0, 384, 640, 896)]
    core = lax.axis_index("core")
    side = 1 - core
    kept_copy = pltpu.make_async_copy(kept_ref, kept_out, out_sems.at[0])
    adopted_copy = pltpu.make_async_copy(adopted_ref, adopted_out, out_sems.at[1])
    for i in range(3):
        adopted_ref[i, :, columns(core)] = half_ref[i]
        kept_ref[i, :, columns(core)] = own_ref[2 * i : 2 * i + 2, :]
        kept_ref[i, :, columns(side)] = other_ref[2 * i : 2 * i + 2, :]
    kept_copy.start()

    def at(start, size):
        return pl.ds(pl.multiple_of(side * HALF + start, 128), size)

    place_half(views, key_ref, weights_ref, adopted_ref, at, adopted_copy.start, rows_ref, sems, core, side)
    kept_copy.wait()
    adopted_copy.wait()


def params(mib=40):
    return pltpu.CompilerParams(vmem_limit_bytes=mib * 1024 * 1024)


def shape(dims, dtype):
    return jax.ShapeDtypeStruct(dims, dtype)


def swapped(value):
    return lax.ppermute(value, "core", [(0, 1), (1, 0)])


def to_neighbours(values):
    pairs = [(2 * p + c, 2 * ((p + 1 + 2 * c) % 4) + c) for p in range(4) for c in range(2)]
    return [lax.ppermute(value, (axis, "core"), pairs) for axis, value in zip("xyz", values)]


def from_leaving(value, group):
    return lax.ppermute(value, ("y", "z", "x", "core"), [(96 + rank, 32 * group + rank) for rank in range(32)])


def body(local_grads, master, first, second, new_owner):
    grads = local_grads.reshape(256, 8192)
    vmem = pl.BlockSpec(memory_space=pltpu.VMEM)
    hbm = pl.BlockSpec(memory_space=pltpu.HBM)
    core = lax.axis_index("core")
    got = swapped(lax.dynamic_slice(grads, (0, (1 - core) * HALF), (256, HALF)))
    low, middle = from_leaving(master, 0), from_leaving(first, 1)
    piece = shape((64, 16, 256), BF)
    keep, *to_send = pl.pallas_call(
        add_kernel,
        in_specs=[vmem] * 4,
        out_specs=[vmem] * 4,
        out_shape=[piece] * 4,
        scratch_shapes=[pltpu.VMEM((64, 16, 1024), BF)],
        compiler_params=params(),
        name="add_blocks",
    )(grads, got, low, middle)
    pair = pl.pallas_call(
        pair_kernel,
        in_specs=[vmem] * 5,
        out_specs=vmem,
        out_shape=shape((8, HALF), F32),
        scratch_shapes=[pltpu.VMEM((2, 8192), F32)],
        compiler_params=params(),
        name="pair",
    )(master, first, second, low, middle)
    arrived = to_neighbours(to_send)
    pair = swapped(pair)
    partial, old = pl.pallas_call(
        merge_kernel,
        in_specs=[vmem] * 10,
        out_specs=[vmem] * 2,
        out_shape=[shape((64, 16, 384), BF), shape((16, HALF), F32)],
        scratch_shapes=[pltpu.VMEM((2, 8192), F32), pltpu.VMEM((8, HALF), F32)],
        compiler_params=params(),
        name="merge",
    )(keep, *arrived, master, first, second, low, middle, pair)
    partial = lax.all_to_all(partial, CHIPS, 0, 0, tiled=True)
    payload, own_new, other_new, key = pl.pallas_call(
        adam_kernel,
        in_specs=[vmem] * 3,
        out_specs=[vmem] * 4,
        out_shape=[
            shape((64, 16, 384), BF),
            shape((8, HALF), F32),
            shape((8, HALF), F32),
            shape((1, 256), jnp.int32),
        ],
        scratch_shapes=[pltpu.VMEM((3, 16, 1024), F32)],
        compiler_params=params(),
        name="adam",
    )(partial, old, new_owner.reshape(1, 64))
    other_new = swapped(other_new)
    blocks = lax.all_to_all(payload, CHIPS, 0, 0, tiled=True)
    mine = pl.pallas_call(
        copy_kernel,
        in_specs=[vmem],
        out_specs=vmem,
        out_shape=piece,
        compiler_params=params(),
        name="mine",
    )(blocks)
    pieces = [blocks] + to_neighbours([mine] * 3)
    joined = pl.pallas_call(
        join_kernel,
        in_specs=[vmem] * 4,
        out_specs=vmem,
        out_shape=shape((64, 16, 1152), BF),
        compiler_params=params(),
        name="join",
    )(*pieces)
    other_joined = swapped(joined)
    scratch = [pltpu.VMEM((256, HALF), BF), pltpu.SemaphoreType.DMA((8,))]
    weights, adopted = pl.pallas_call(
        place_own_kernel,
        in_specs=[vmem] * 5,
        out_specs=[hbm, vmem],
        out_shape=[shape((256, 8192), BF), shape((3, 2, HALF), F32)],
        scratch_shapes=scratch,
        compiler_params=params(),
        cost_estimate=pl.CostEstimate(flops=8_000_000, bytes_accessed=8_000_000, transcendentals=0),
        name="place_own",
    )(*pieces, key)
    weights, adopted, kept = pl.pallas_call(
        place_other_kernel,
        in_specs=[vmem] * 2 + [hbm] + [vmem] * 3,
        out_specs=[hbm] * 3,
        out_shape=[shape((256, 8192), BF), shape((3, 2, 8192), F32), shape((3, 2, 8192), F32)],
        scratch_shapes=[pltpu.VMEM((3, 2, 8192), F32)] * 2 + scratch + [pltpu.SemaphoreType.DMA((2,))],
        input_output_aliases={2: 0},
        compiler_params=params(),
        name="place_other",
    )(other_joined, key, weights, adopted, own_new, other_new)
    return (weights, kept.transpose(1, 0, 2), adopted.transpose(1, 0, 2)[None, None])


def solution(mesh):
    fine = Mesh(mesh.devices.reshape(4, 4, 4, 2), ("y", "z", "x", "core"))
    every = ("y", "z", "x", "core")
    in_specs = (P("y", ("z", "x", "core"), None, None), P(every, None), P(every, None), P(every, None), P())
    out_specs = (P(), P(every, None, None), P("y", ("z", "x", "core"), None, None, None))
    return jax.shard_map(body, mesh=fine, in_specs=in_specs, out_specs=out_specs, check_vma=False)
```

```python
import jax
import jax.numpy as jnp
from jax import lax
from jax.experimental import pallas as pl
from jax.experimental.pallas import tpu as pltpu
from jax.sharding import Mesh
from jax.sharding import PartitionSpec as P

ADAM_STEP = 20

beta_one = 0.9
beta_two = 0.95
learn_rate = 0.05
epsilon = 1e-08

CHIPS = ("y", "z", "x")
BF = jnp.bfloat16
F32 = jnp.float32
HALF = 4096


def adam_update(master, first, second, gradient):
    first_new = beta_one * first + (1.0 - beta_one) * gradient
    second_new = beta_two * second + (1.0 - beta_two) * gradient * gradient
    corr_one = 1.0 - beta_one**ADAM_STEP
    corr_two = 1.0 - beta_two**ADAM_STEP
    master_new = master - learn_rate * (first_new / corr_one) / (
        jnp.sqrt(second_new / corr_two) + epsilon
    )
    return (master_new, first_new, second_new)


def iota(shape, dim):
    return lax.broadcasted_iota(jnp.int32, shape, dim)


def one_hot(target):
    return jnp.where(iota(target.shape, 1) == target, 1.0, 0.0).astype(BF)


def pick(matrix, values):
    return jnp.dot(matrix, values, preferred_element_type=F32)


def columns(core):
    return pl.ds(pl.multiple_of(core * HALF, HALF), HALF)


def turned(rows):
    return pltpu.roll(rows, 4, axis=0)


def spread_rows(low_ref, middle_ref, second_ref):
    y = lax.axis_index("y")
    return jnp.where(y == 0, low_ref[...], jnp.where(y == 2, middle_ref[...], second_ref[...]))


def pair_kernel(master_ref, first_ref, second_ref, low_ref, middle_ref, pair_ref, rows_ref):
    other = columns(1 - lax.axis_index("core"))
    for i, ref in enumerate((master_ref, first_ref, second_ref)):
        pair_ref[2 * i : 2 * i + 2, :] = ref[:, other]
    rows_ref[...] = spread_rows(low_ref, middle_ref, second_ref)
    pair_ref[6:8, :] = rows_ref[:, other]


def chip_class(chip):
    return (chip & 1) ^ (((chip >> 4) & 1) * 2) ^ (((chip >> 2) & 1) * 3)


def own_chip():
    return (lax.axis_index("y") * 4 + lax.axis_index("z")) * 4 + lax.axis_index("x")


def quarter(number):
    return pl.ds(pl.multiple_of(number * 256, 256), 256)


def add_kernel(
    grads_ref, got_ref, low_ref, middle_ref, keep_ref, x_ref, y_ref, z_ref, blocks_ref
):
    core = lax.axis_index("core")
    low = iota((8, 1024), 0) < 4

    def kept(i, carry):
        rows = pl.ds(pl.multiple_of(16 * i, 16), 16)
        parts = []
        for k in range(4):
            cut = pl.ds(pl.multiple_of(core * HALF + k * 1024, 1024), 1024)
            got = got_ref[rows, k * 1024 : (k + 1) * 1024]
            parts.append(grads_ref[rows, cut].astype(F32) + got.astype(F32))
        for tile in range(2):
            c = [part[8 * tile : 8 * tile + 8] for part in parts]
            even = [jnp.where(low, c[k], turned(c[k + 1])) for k in (0, 2)]
            odd = [jnp.where(low, turned(c[k]), c[k + 1]) for k in (0, 2)]
            for chip, block in ((4 * i + 2 * tile, even), (4 * i + 2 * tile + 1, odd)):
                blocks_ref[chip] = jnp.concatenate(block, axis=0).astype(BF)
        return carry

    lax.fori_loop(0, 12, kept, 0)

    def leave(q, carry):
        cut = pl.ds(pl.multiple_of(q * 256, 256), 256)
        own_cut = pl.ds(pl.multiple_of(core * HALF + q * 256, 256), 256)
        for a in range(4):
            rows = slice(192 + 16 * a, 208 + 16 * a)
            total = grads_ref[rows, own_cut].astype(F32) + got_ref[rows, cut].astype(F32)
            blocks_ref[48 + q, :, a * 256 : (a + 1) * 256] = total.astype(BF)
        return carry

    lax.fori_loop(0, 16, leave, 0)
    kind = chip_class(own_chip())
    keep_ref[...] = blocks_ref[:, :, quarter(kind)]
    for axis, ref in enumerate((x_ref, y_ref, z_ref)):
        ref[...] = blocks_ref[:, :, quarter(kind ^ (axis + 1))]


def merge_kernel(
    keep_ref, x_ref, y_ref, z_ref,
    master_ref, first_ref, second_ref, low_ref, middle_ref, pair_ref,
    out_ref, old_ref, rows_ref, split_ref,
):
    core = lax.axis_index("core")

    def add(d, carry):
        total = keep_ref[d].astype(F32)
        for ref in (x_ref, y_ref, z_ref):
            total = total + ref[d].astype(F32)
        out_ref[d, :, 0:256] = total.astype(BF)
        return carry

    lax.fori_loop(0, 64, add, 0, unroll=8)

    rows_ref[...] = spread_rows(low_ref, middle_ref, second_ref)
    for mine in range(2):

        @pl.when(core == mine)
        def _():
            for i, ref in enumerate((master_ref, first_ref, second_ref, rows_ref)):
                at = 4 * i + 2 * mine
                old_ref[at : at + 2, :] = ref[:, mine * HALF : (mine + 1) * HALF]
                at = 4 * i + 2 * (1 - mine)
                old_ref[at : at + 2, :] = pair_ref[2 * i : 2 * i + 2, :]

    passed = old_ref[12:16, :]
    high = passed.astype(BF).astype(F32)
    split_ref[0:4, :] = high
    split_ref[4:8, :] = passed - high

    def empty(d, carry):
        out_ref[d, :, 256:384] = jnp.zeros((16, 128), BF)
        return carry

    lax.fori_loop(0, 48, empty, 0, unroll=8)

    def leave(q, carry):
        parts = split_ref[:, quarter(q)]
        out_ref[48 + q, :, 256:384] = jnp.concatenate([parts[:, 0:128], parts[:, 128:256]], axis=0).astype(BF)
        return carry

    lax.fori_loop(0, 16, leave, 0, unroll=4)


def adam_kernel(parts_ref, chip_ref, owner_ref, out_ref, own_ref, other_ref, key_ref, old_ref):
    leaving = lax.axis_index("y") == 3
    core = lax.axis_index("core")
    totals = [jnp.zeros((16, 256), F32)] * 4
    for chip in range(64):
        kind = chip_class(chip)
        totals[kind] = totals[kind] + parts_ref[chip, :, 0:256].astype(F32)
    gradient = jnp.concatenate(totals, axis=1)

    @pl.when(leaving)
    def _():
        for i, y in enumerate((0, 2, 3)):
            for q in range(16):
                parts = parts_ref[16 * y + q, :, 256:384].astype(F32)
                for h in range(2):
                    value = parts[8 * h : 8 * h + 4] + parts[8 * h + 4 : 8 * h + 8]
                    at = (q // 4) * 256 + h * 128
                    old_ref[i, 4 * (q % 4) : 4 * (q % 4) + 4, at : at + 128] = value

    @pl.when(jnp.logical_not(leaving))
    def _():
        for i in range(3):
            for k in range(4):
                old_ref[i, 4 * k : 4 * k + 4, :] = chip_ref[4 * i : 4 * i + 4, k * 1024 : (k + 1) * 1024]

    new = adam_update(old_ref[0], old_ref[1], old_ref[2], gradient)
    own_ref[6:8, :] = jnp.zeros((2, HALF), F32)
    other_ref[6:8, :] = jnp.zeros((2, HALF), F32)
    values = [jnp.where(leaving, jnp.zeros_like(value), value) for value in new]
    for mine in range(2):

        @pl.when(core == mine)
        def _():
            for i in range(3):
                for k in range(4):
                    cut = slice(k * 1024, (k + 1) * 1024)
                    at = 4 * k + 2 * mine
                    own_ref[2 * i : 2 * i + 2, cut] = values[i][at : at + 2, :]
                    at = 4 * k + 2 * (1 - mine)
                    other_ref[2 * i : 2 * i + 2, cut] = values[i][at : at + 2, :]

    weights = new[0].astype(BF)

    for chip in range(64):
        kind = chip_class(chip)
        out_ref[chip, :, 0:256] = weights[:, kind * 256 : (kind + 1) * 256]

    lane, row = iota((64, 256), 1), iota((64, 256), 0)
    tiled = jnp.where((lane & 63) == row, 1.0, 0.0).astype(BF)
    across = pick(jnp.broadcast_to(owner_ref[...], (64, 64)).astype(F32).astype(BF), tiled)
    down = jnp.sum(jnp.where(lane == row, across, 0.0), axis=1, keepdims=True)
    earlier = (across == down) & (row < (lane & 63))
    slot = jnp.sum(jnp.where(earlier, 1.0, 0.0), axis=0, keepdims=True)
    key = (across[0:1, :] * 2.0 + slot).astype(jnp.int32) + 512 * (iota((1, 256), 1) >> 6)
    key_ref[...] = key
    moments = jnp.concatenate(
        [
            new[1 + part // 2][:, a * 256 + (part % 2) * 128 : a * 256 + (part % 2) * 128 + 128]
            for part in range(4)
            for a in range(4)
        ],
        axis=0,
    ).astype(BF)
    p = iota((1024, 256), 0)
    wanted = (p >> 4) * 4 + (p & 3) + 512 * ((p >> 2) & 3)
    chosen = jnp.where(key == wanted, 1.0, 0.0).astype(BF)
    out_ref[:, :, 256:384] = pick(chosen, moments).astype(BF).reshape(64, 16, 128)


def copy_kernel(blocks_ref, out_ref):
    out_ref[...] = blocks_ref[:, :, 0:256]


def place_half(views, key_ref, weights_ref, adopted_ref, adopted_at, adopted_ready, rows_ref, sems, core, side):
    blocks_ref = views[0][0]
    chip = own_chip()
    kind = chip_class(chip)
    low = iota((8, 256), 0) < 4

    def store(i):
        rows = pl.ds(pl.multiple_of(32 * i, 32), 32)
        return pltpu.make_async_copy(rows_ref.at[rows, :], weights_ref.at[rows, columns(side)], sems.at[i])

    def kept(i, carry):
        for axis in range(4):
            ref, lane = views[axis]
            for g in range(2):
                tiles = []
                for tile in range(2):
                    number = 8 * i + 4 * g + 2 * tile
                    even = ref[number, :, lane : lane + 256].astype(F32)
                    odd = ref[number + 1, :, lane : lane + 256].astype(F32)
                    cut = []
                    for s in (slice(0, 8), slice(8, 16)):
                        cut.append(jnp.where(low, even[s], turned(odd[s])))
                        cut.append(jnp.where(low, turned(even[s]), odd[s]))
                    tiles.append(cut)
                rows = pl.ds(pl.multiple_of(32 * i + 16 * g, 16), 16)
                for k in range(4):
                    rows_ref[rows, quarter((kind ^ axis) + 4 * k)] = jnp.concatenate(
                        [tiles[0][k], tiles[1][k]], axis=0
                    ).astype(BF)
        store(i).start()
        return carry

    for axis in range(4):
        ref, lane = views[axis]
        rows = pl.ds(pl.multiple_of(192 + 16 * (kind ^ axis), 16), 16)
        for q in range(16):
            rows_ref[rows, q * 256 : (q + 1) * 256] = ref[48 + q, :, lane : lane + 256]
    for i in range(6, 8):
        store(i).start()
    k = iota((8, 64), 0)
    wanted = jnp.where(k < 2, chip * 4 + core * 2 + k, -1)
    chosen = jnp.where(key_ref[:, 0:64] == wanted, 1.0, 0.0).astype(BF)
    masters = pick(chosen, rows_ref[192:256, :])
    adopted_ref[0, :, adopted_at(0, HALF)] = masters[0:2, :]
    moments = jnp.concatenate([blocks_ref[48 + q, :, 256:384] for q in range(16)], axis=1)
    for h in range(2):
        k = iota((8, 16), 0)
        found = pick(one_hot(jnp.where(k < 4, ((k >> 1) * 2 + h) * 4 + core * 2 + (k & 1), -1)), moments)
        for q in range(16):
            for i in range(2):
                adopted_ref[1 + i, :, adopted_at(q * 256 + h * 128, 128)] = found[
                    2 * i : 2 * i + 2, q * 128 : (q + 1) * 128
                ]
    adopted_ready()
    lax.fori_loop(0, 6, kept, 0)
    for i in range(8):
        store(i).wait()


def place_own_kernel(
    blocks_ref, x_ref, y_ref, z_ref, key_ref, weights_ref, adopted_ref, rows_ref, sems
):
    views = [(ref, 0) for ref in (blocks_ref, x_ref, y_ref, z_ref)]
    core = lax.axis_index("core")
    place_half(
        views, key_ref, weights_ref, adopted_ref, lambda start, size: slice(start, start + size), lambda: None,
        rows_ref, sems, core, core,
    )


def place_other_kernel(*refs):
    key_ref, _, half_ref, own_ref, other_ref = refs[4:9]
    weights_ref, adopted_out, kept_out, adopted_ref, kept_ref, rows_ref, sems, out_sems = refs[9:]
    views = [(ref, 0) for ref in refs[:4]]
    core = lax.axis_index("core")
    side = 1 - core
    kept_copy = pltpu.make_async_copy(kept_ref, kept_out, out_sems.at[0])
    adopted_copy = pltpu.make_async_copy(adopted_ref, adopted_out, out_sems.at[1])
    for i in range(3):
        adopted_ref[i, :, columns(core)] = half_ref[i]
        kept_ref[i, :, columns(core)] = own_ref[2 * i : 2 * i + 2, :]
        kept_ref[i, :, columns(side)] = other_ref[2 * i : 2 * i + 2, :]
    kept_copy.start()

    def at(start, size):
        return pl.ds(pl.multiple_of(side * HALF + start, 128), size)

    place_half(views, key_ref, weights_ref, adopted_ref, at, adopted_copy.start, rows_ref, sems, core, side)
    kept_copy.wait()
    adopted_copy.wait()


def params(mib=40):
    return pltpu.CompilerParams(vmem_limit_bytes=mib * 1024 * 1024)


def shape(dims, dtype):
    return jax.ShapeDtypeStruct(dims, dtype)


def swapped(value):
    return lax.ppermute(value, "core", [(0, 1), (1, 0)])


def to_neighbours(values):
    pairs = [(2 * p + c, 2 * ((p + 1 + 2 * c) % 4) + c) for p in range(4) for c in range(2)]
    return [lax.ppermute(value, (axis, "core"), pairs) for axis, value in zip("xyz", values)]


def from_leaving(value, group):
    return lax.ppermute(value, ("y", "z", "x", "core"), [(96 + rank, 32 * group + rank) for rank in range(32)])


def body(local_grads, master, first, second, new_owner):
    grads = local_grads.reshape(256, 8192)
    vmem = pl.BlockSpec(memory_space=pltpu.VMEM)
    hbm = pl.BlockSpec(memory_space=pltpu.HBM)
    core = lax.axis_index("core")
    got = swapped(lax.dynamic_slice(grads, (0, (1 - core) * HALF), (256, HALF)))
    low, middle = from_leaving(master, 0), from_leaving(first, 2)
    piece = shape((64, 16, 256), BF)
    keep, *to_send = pl.pallas_call(
        add_kernel,
        in_specs=[vmem] * 4,
        out_specs=[vmem] * 4,
        out_shape=[piece] * 4,
        scratch_shapes=[pltpu.VMEM((64, 16, 1024), BF)],
        compiler_params=params(),
        name="add_blocks",
    )(grads, got, low, middle)
    pair = pl.pallas_call(
        pair_kernel,
        in_specs=[vmem] * 5,
        out_specs=vmem,
        out_shape=shape((8, HALF), F32),
        scratch_shapes=[pltpu.VMEM((2, 8192), F32)],
        compiler_params=params(),
        name="pair",
    )(master, first, second, low, middle)
    arrived = to_neighbours(to_send)
    pair = swapped(pair)
    partial, old = pl.pallas_call(
        merge_kernel,
        in_specs=[vmem] * 10,
        out_specs=[vmem] * 2,
        out_shape=[shape((64, 16, 384), BF), shape((16, HALF), F32)],
        scratch_shapes=[pltpu.VMEM((2, 8192), F32), pltpu.VMEM((8, HALF), F32)],
        compiler_params=params(),
        name="merge",
    )(keep, *arrived, master, first, second, low, middle, pair)
    partial = lax.all_to_all(partial, CHIPS, 0, 0, tiled=True)
    payload, own_new, other_new, key = pl.pallas_call(
        adam_kernel,
        in_specs=[vmem] * 3,
        out_specs=[vmem] * 4,
        out_shape=[
            shape((64, 16, 384), BF),
            shape((8, HALF), F32),
            shape((8, HALF), F32),
            shape((1, 256), jnp.int32),
        ],
        scratch_shapes=[pltpu.VMEM((3, 16, 1024), F32)],
        compiler_params=params(),
        name="adam",
    )(partial, old, new_owner.reshape(1, 64))
    other_new = swapped(other_new)
    blocks = lax.all_to_all(payload, CHIPS, 0, 0, tiled=True)
    mine = pl.pallas_call(
        copy_kernel,
        in_specs=[vmem],
        out_specs=vmem,
        out_shape=piece,
        compiler_params=params(),
        name="mine",
    )(blocks)
    pieces = [blocks] + to_neighbours([mine] * 3)
    other_pieces = [swapped(value) for value in pieces]
    scratch = [pltpu.VMEM((256, HALF), BF), pltpu.SemaphoreType.DMA((8,))]
    weights, adopted = pl.pallas_call(
        place_own_kernel,
        in_specs=[vmem] * 5,
        out_specs=[hbm, vmem],
        out_shape=[shape((256, 8192), BF), shape((3, 2, HALF), F32)],
        scratch_shapes=scratch,
        compiler_params=params(),
        cost_estimate=pl.CostEstimate(flops=8_000_000, bytes_accessed=8_000_000, transcendentals=0),
        name="place_own",
    )(*pieces, key)
    weights, adopted, kept = pl.pallas_call(
        place_other_kernel,
        in_specs=[vmem] * 5 + [hbm] + [vmem] * 3,
        out_specs=[hbm] * 3,
        out_shape=[shape((256, 8192), BF), shape((3, 2, 8192), F32), shape((3, 2, 8192), F32)],
        scratch_shapes=[pltpu.VMEM((3, 2, 8192), F32)] * 2 + scratch + [pltpu.SemaphoreType.DMA((2,))],
        input_output_aliases={5: 0},
        compiler_params=params(),
        name="place_other",
    )(*other_pieces, key, weights, adopted, own_new, other_new)
    return (weights, kept.transpose(1, 0, 2), adopted.transpose(1, 0, 2)[None, None])


def solution(mesh):
    fine = Mesh(mesh.devices.reshape(4, 4, 4, 2), ("y", "z", "x", "core"))
    every = ("y", "z", "x", "core")
    in_specs = (P("y", ("z", "x", "core"), None, None), P(every, None), P(every, None), P(every, None), P())
    out_specs = (P(), P(every, None, None), P("y", ("z", "x", "core"), None, None, None))
    return jax.shard_map(body, mesh=fine, in_specs=in_specs, out_specs=out_specs, check_vma=False)
```

```python
import jax
import jax.numpy as jnp
from jax import lax
from jax.experimental import pallas as pl
from jax.experimental.pallas import tpu as pltpu
from jax.sharding import Mesh
from jax.sharding import PartitionSpec as P

ADAM_STEP = 20

beta_one = 0.9
beta_two = 0.95
learn_rate = 0.05
epsilon = 1e-08

CHIPS = ("y", "z", "x")
BF = jnp.bfloat16
F32 = jnp.float32
HALF = 4096


def adam_update(master, first, second, gradient):
    first_new = beta_one * first + (1.0 - beta_one) * gradient
    second_new = beta_two * second + (1.0 - beta_two) * gradient * gradient
    corr_one = 1.0 - beta_one**ADAM_STEP
    corr_two = 1.0 - beta_two**ADAM_STEP
    master_new = master - learn_rate * (first_new / corr_one) / (
        jnp.sqrt(second_new / corr_two) + epsilon
    )
    return (master_new, first_new, second_new)


def iota(shape, dim):
    return lax.broadcasted_iota(jnp.int32, shape, dim)


def one_hot(target):
    return jnp.where(iota(target.shape, 1) == target, 1.0, 0.0).astype(BF)


def pick(matrix, values):
    return jnp.dot(matrix, values, preferred_element_type=F32)


def columns(core):
    return pl.ds(pl.multiple_of(core * HALF, HALF), HALF)


def turned(rows):
    return pltpu.roll(rows, 4, axis=0)


def stack_kernel(master_ref, first_ref, out_ref):
    out_ref[0:2, :] = master_ref[...]
    out_ref[2:4, :] = first_ref[...]


def pair_kernel(master_ref, first_ref, second_ref, passed_ref, pair_ref):
    other = columns(1 - lax.axis_index("core"))
    pair_ref[...] = jnp.zeros_like(pair_ref)
    for i, ref in enumerate((master_ref, first_ref, second_ref)):
        pair_ref[2 * i : 2 * i + 2, :] = ref[:, other]
    pair_ref[8:12, :] = passed_ref[:, other]


def chip_class(chip):
    return (chip & 1) ^ (((chip >> 4) & 1) * 2) ^ (((chip >> 2) & 1) * 3)


def own_chip():
    return (lax.axis_index("y") * 4 + lax.axis_index("z")) * 4 + lax.axis_index("x")


def quarter(number):
    return pl.ds(pl.multiple_of(number * 256, 256), 256)


def add_kernel(
    grads_ref, got_ref, passed_ref, keep_ref, x_ref, y_ref, z_ref
):
    core = lax.axis_index("core")
    kind = chip_class(own_chip())
    low = iota((8, 256), 0) < 4
    pieces = (keep_ref, x_ref, y_ref, z_ref)

    def kept(i, carry):
        rows = pl.ds(pl.multiple_of(16 * i, 16), 16)
        for axis, ref in enumerate(pieces):
            parts = []
            for k in range(4):
                at = (kind ^ axis) * 4 + k
                parts.append(grads_ref[rows, quarter(core * 16 + at)].astype(F32) + got_ref[rows, quarter(at)].astype(F32))
            for tile in range(2):
                c = [part[8 * tile : 8 * tile + 8] for part in parts]
                even = [jnp.where(low, c[k], turned(c[k + 1])) for k in (0, 2)]
                odd = [jnp.where(low, turned(c[k]), c[k + 1]) for k in (0, 2)]
                for chip, block in ((4 * i + 2 * tile, even), (4 * i + 2 * tile + 1, odd)):
                    ref[chip] = jnp.concatenate(block, axis=0).astype(BF)
        return carry

    lax.fori_loop(0, 12, kept, 0)

    def leave(q, carry):
        for axis, ref in enumerate(pieces):
            rows = pl.ds(pl.multiple_of(192 + 16 * (kind ^ axis), 16), 16)
            total = grads_ref[rows, quarter(core * 16 + q)].astype(F32) + got_ref[rows, quarter(q)].astype(F32)
            ref[48 + q] = total.astype(BF)
        return carry

    lax.fori_loop(0, 16, leave, 0, unroll=4)


def merge_kernel(
    keep_ref, x_ref, y_ref, z_ref,
    master_ref, first_ref, second_ref, passed_ref, pair_ref, out_ref, old_ref, split_ref,
):
    core = lax.axis_index("core")

    def add(d, carry):
        total = keep_ref[d].astype(F32)
        for ref in (x_ref, y_ref, z_ref):
            total = total + ref[d].astype(F32)
        out_ref[d, :, 0:256] = total.astype(BF)
        return carry

    lax.fori_loop(0, 64, add, 0, unroll=8)

    old_ref[12:16, :] = jnp.zeros((4, HALF), F32)
    for mine in range(2):

        @pl.when(core == mine)
        def _():
            for i, ref in enumerate((master_ref, first_ref, second_ref)):
                at = 4 * i + 2 * mine
                old_ref[at : at + 2, :] = ref[:, mine * HALF : (mine + 1) * HALF]
                at = 4 * i + 2 * (1 - mine)
                old_ref[at : at + 2, :] = pair_ref[2 * i : 2 * i + 2, :]

    passed = passed_ref[:, columns(core)] + pair_ref[8:12, :]
    passed = jnp.where(lax.axis_index("y") == 3, old_ref[8:12, :], passed)
    high = passed.astype(BF).astype(F32)
    split_ref[0:4, :] = high
    split_ref[4:8, :] = passed - high

    def empty(d, carry):
        out_ref[d, :, 256:384] = jnp.zeros((16, 128), BF)
        return carry

    lax.fori_loop(0, 48, empty, 0, unroll=8)

    def leave(q, carry):
        parts = split_ref[:, quarter(q)]
        out_ref[48 + q, :, 256:384] = jnp.concatenate([parts[:, 0:128], parts[:, 128:256]], axis=0).astype(BF)
        return carry

    lax.fori_loop(0, 16, leave, 0, unroll=4)


def adam_kernel(parts_ref, chip_ref, owner_ref, out_ref, own_ref, other_ref, key_ref, old_ref):
    leaving = lax.axis_index("y") == 3
    core = lax.axis_index("core")
    totals = [jnp.zeros((16, 256), F32)] * 4
    for chip in range(64):
        kind = chip_class(chip)
        totals[kind] = totals[kind] + parts_ref[chip, :, 0:256].astype(F32)
    gradient = jnp.concatenate(totals, axis=1)

    @pl.when(leaving)
    def _():
        for y in (0, 2, 3):
            for q in range(16):
                parts = parts_ref[16 * y + q, :, 256:384].astype(F32)
                row = 4 * (q % 4)
                for h in range(2):
                    value = parts[8 * h : 8 * h + 4] + parts[8 * h + 4 : 8 * h + 8]
                    cut = slice((q // 4) * 256 + h * 128, (q // 4) * 256 + h * 128 + 128)
                    if y == 3:
                        old_ref[2, row : row + 4, cut] = value
                    else:
                        old_ref[0, row + y : row + y + 2, cut] = value[0:2]
                        old_ref[1, row + y : row + y + 2, cut] = value[2:4]

    @pl.when(jnp.logical_not(leaving))
    def _():
        for i in range(3):
            for n in range(16):
                k, u = n % 4, n // 4
                old_ref[i, 4 * k : 4 * k + 4, u * 256 : (u + 1) * 256] = chip_ref[
                    4 * i : 4 * i + 4, n * 256 : (n + 1) * 256
                ]

    new = adam_update(old_ref[0], old_ref[1], old_ref[2], gradient)
    own_ref[6:8, :] = jnp.zeros((2, HALF), F32)
    other_ref[6:8, :] = jnp.zeros((2, HALF), F32)
    values = [jnp.where(leaving, jnp.zeros_like(value), value) for value in new]
    for mine in range(2):

        @pl.when(core == mine)
        def _():
            for i in range(3):
                for n in range(16):
                    k, u = n % 4, n // 4
                    cut, lanes = slice(n * 256, (n + 1) * 256), slice(u * 256, (u + 1) * 256)
                    at = 4 * k + 2 * mine
                    own_ref[2 * i : 2 * i + 2, cut] = values[i][at : at + 2, lanes]
                    at = 4 * k + 2 * (1 - mine)
                    other_ref[2 * i : 2 * i + 2, cut] = values[i][at : at + 2, lanes]

    weights = new[0].astype(BF)

    for chip in range(64):
        kind = chip_class(chip)
        out_ref[chip, :, 0:256] = weights[:, kind * 256 : (kind + 1) * 256]

    lane, row = iota((64, 256), 1), iota((64, 256), 0)
    tiled = jnp.where((lane & 63) == row, 1.0, 0.0).astype(BF)
    across = pick(jnp.broadcast_to(owner_ref[...], (64, 64)).astype(F32).astype(BF), tiled)
    down = jnp.sum(jnp.where(lane == row, across, 0.0), axis=1, keepdims=True)
    earlier = (across == down) & (row < (lane & 63))
    slot = jnp.sum(jnp.where(earlier, 1.0, 0.0), axis=0, keepdims=True)
    key = (across[0:1, :] * 2.0 + slot).astype(jnp.int32) + 512 * (iota((1, 256), 1) >> 6)
    key_ref[...] = key
    moments = jnp.concatenate(
        [
            new[1 + part // 2][:, a * 256 + (part % 2) * 128 : a * 256 + (part % 2) * 128 + 128]
            for part in range(4)
            for a in range(4)
        ],
        axis=0,
    ).astype(BF)
    p = iota((1024, 256), 0)
    wanted = (p >> 4) * 4 + (p & 3) + 512 * ((p >> 2) & 3)
    chosen = jnp.where(key == wanted, 1.0, 0.0).astype(BF)
    out_ref[:, :, 256:384] = pick(chosen, moments).astype(BF).reshape(64, 16, 128)


def copy_kernel(blocks_ref, out_ref):
    out_ref[...] = blocks_ref[:, :, 0:256]


def place_half(views, key_ref, weights_ref, adopted_ref, adopted_at, adopted_ready, rows_ref, sems, core, side):
    blocks_ref = views[0][0]
    chip = own_chip()
    kind = chip_class(chip)
    low = iota((8, 256), 0) < 4

    def store(i):
        rows = pl.ds(pl.multiple_of(32 * i, 32), 32)
        return pltpu.make_async_copy(rows_ref.at[rows, :], weights_ref.at[rows, columns(side)], sems.at[i])

    def kept(i, carry):
        for axis in range(4):
            ref, lane = views[axis]
            for g in range(2):
                tiles = []
                for tile in range(2):
                    number = 8 * i + 4 * g + 2 * tile
                    even = ref[number, :, lane : lane + 256].astype(F32)
                    odd = ref[number + 1, :, lane : lane + 256].astype(F32)
                    cut = []
                    for s in (slice(0, 8), slice(8, 16)):
                        cut.append(jnp.where(low, even[s], turned(odd[s])))
                        cut.append(jnp.where(low, turned(even[s]), odd[s]))
                    tiles.append(cut)
                rows = pl.ds(pl.multiple_of(32 * i + 16 * g, 16), 16)
                for k in range(4):
                    rows_ref[rows, quarter((kind ^ axis) * 4 + k)] = jnp.concatenate(
                        [tiles[0][k], tiles[1][k]], axis=0
                    ).astype(BF)
        store(i).start()
        return carry

    for axis in range(4):
        ref, lane = views[axis]
        rows = pl.ds(pl.multiple_of(192 + 16 * (kind ^ axis), 16), 16)
        for q in range(16):
            rows_ref[rows, q * 256 : (q + 1) * 256] = ref[48 + q, :, lane : lane + 256]
    for i in range(6, 8):
        store(i).start()
    k = iota((8, 64), 0)
    wanted = jnp.where(k < 2, chip * 4 + core * 2 + k, -1)
    chosen = jnp.where(key_ref[:, 0:64] == wanted, 1.0, 0.0).astype(BF)
    masters = pick(chosen, rows_ref[192:256, :])
    adopted_ref[0, :, adopted_at(0, HALF)] = masters[0:2, :]
    moments = jnp.concatenate([blocks_ref[48 + q, :, 256:384] for q in range(16)], axis=1)
    for h in range(2):
        k = iota((8, 16), 0)
        found = pick(one_hot(jnp.where(k < 4, ((k >> 1) * 2 + h) * 4 + core * 2 + (k & 1), -1)), moments)
        for q in range(16):
            for i in range(2):
                adopted_ref[1 + i, :, adopted_at(q * 256 + h * 128, 128)] = found[
                    2 * i : 2 * i + 2, q * 128 : (q + 1) * 128
                ]
    adopted_ready()
    lax.fori_loop(0, 6, kept, 0)
    for i in range(8):
        store(i).wait()


def place_own_kernel(
    blocks_ref, x_ref, y_ref, z_ref, key_ref, weights_ref, adopted_ref, rows_ref, sems
):
    views = [(ref, 0) for ref in (blocks_ref, x_ref, y_ref, z_ref)]
    core = lax.axis_index("core")
    place_half(
        views, key_ref, weights_ref, adopted_ref, lambda start, size: slice(start, start + size), lambda: None,
        rows_ref, sems, core, core,
    )


def place_other_kernel(*refs):
    key_ref, _, half_ref, own_ref, other_ref = refs[4:9]
    weights_ref, adopted_out, kept_out, adopted_ref, kept_ref, rows_ref, sems, out_sems = refs[9:]
    views = [(ref, 0) for ref in refs[:4]]
    core = lax.axis_index("core")
    side = 1 - core
    kept_copy = pltpu.make_async_copy(kept_ref, kept_out, out_sems.at[0])
    adopted_copy = pltpu.make_async_copy(adopted_ref, adopted_out, out_sems.at[1])
    for i in range(3):
        adopted_ref[i, :, columns(core)] = half_ref[i]
        kept_ref[i, :, columns(core)] = own_ref[2 * i : 2 * i + 2, :]
        kept_ref[i, :, columns(side)] = other_ref[2 * i : 2 * i + 2, :]
    kept_copy.start()

    def at(start, size):
        return pl.ds(pl.multiple_of(side * HALF + start, 128), size)

    place_half(views, key_ref, weights_ref, adopted_ref, at, adopted_copy.start, rows_ref, sems, core, side)
    kept_copy.wait()
    adopted_copy.wait()


def params(mib=40):
    return pltpu.CompilerParams(vmem_limit_bytes=mib * 1024 * 1024)


def shape(dims, dtype):
    return jax.ShapeDtypeStruct(dims, dtype)


def swapped(value):
    return lax.ppermute(value, "core", [(0, 1), (1, 0)])


def to_neighbours(values):
    pairs = [(2 * p + c, 2 * ((p + 1 + 2 * c) % 4) + c) for p in range(4) for c in range(2)]
    return [lax.ppermute(value, (axis, "core"), pairs) for axis, value in zip("xyz", values)]


def from_leaving(value):
    pairs = [(96 + rank, 64 * (rank % 2) + rank) for rank in range(32)]
    return lax.ppermute(value, ("y", "z", "x", "core"), pairs)


def body(local_grads, master, first, second, new_owner):
    grads = local_grads.reshape(256, 8192)
    vmem = pl.BlockSpec(memory_space=pltpu.VMEM)
    hbm = pl.BlockSpec(memory_space=pltpu.HBM)
    core = lax.axis_index("core")
    got = swapped(lax.dynamic_slice(grads, (0, (1 - core) * HALF), (256, HALF)))
    stacked = pl.pallas_call(
        stack_kernel,
        in_specs=[vmem] * 2,
        out_specs=vmem,
        out_shape=shape((4, 8192), F32),
        compiler_params=params(),
        name="stack",
    )(master, first)
    passed = from_leaving(stacked)
    piece = shape((64, 16, 256), BF)
    keep, *to_send = pl.pallas_call(
        add_kernel,
        in_specs=[vmem] * 3,
        out_specs=[vmem] * 4,
        out_shape=[piece] * 4,
        compiler_params=params(),
        name="add_blocks",
    )(grads, got, passed)
    pair = pl.pallas_call(
        pair_kernel,
        in_specs=[vmem] * 4,
        out_specs=vmem,
        out_shape=shape((16, HALF), F32),
        compiler_params=params(),
        name="pair",
    )(master, first, second, passed)
    arrived = to_neighbours(to_send)
    pair = swapped(pair)
    partial, old = pl.pallas_call(
        merge_kernel,
        in_specs=[vmem] * 9,
        out_specs=[vmem] * 2,
        out_shape=[shape((64, 16, 384), BF), shape((16, HALF), F32)],
        scratch_shapes=[pltpu.VMEM((8, HALF), F32)],
        compiler_params=params(),
        name="merge",
    )(keep, *arrived, master, first, second, passed, pair)
    partial = lax.all_to_all(partial, CHIPS, 0, 0, tiled=True)
    payload, own_new, other_new, key = pl.pallas_call(
        adam_kernel,
        in_specs=[vmem] * 3,
        out_specs=[vmem] * 4,
        out_shape=[
            shape((64, 16, 384), BF),
            shape((8, HALF), F32),
            shape((8, HALF), F32),
            shape((1, 256), jnp.int32),
        ],
        scratch_shapes=[pltpu.VMEM((3, 16, 1024), F32)],
        compiler_params=params(),
        name="adam",
    )(partial, old, new_owner.reshape(1, 64))
    other_new = swapped(other_new)
    blocks = lax.all_to_all(payload, CHIPS, 0, 0, tiled=True)
    mine = pl.pallas_call(
        copy_kernel,
        in_specs=[vmem],
        out_specs=vmem,
        out_shape=piece,
        compiler_params=params(),
        name="mine",
    )(blocks)
    pieces = [blocks] + to_neighbours([mine] * 3)
    other_pieces = [swapped(value) for value in pieces]
    scratch = [pltpu.VMEM((256, HALF), BF), pltpu.SemaphoreType.DMA((8,))]
    weights, adopted = pl.pallas_call(
        place_own_kernel,
        in_specs=[vmem] * 5,
        out_specs=[hbm, vmem],
        out_shape=[shape((256, 8192), BF), shape((3, 2, HALF), F32)],
        scratch_shapes=scratch,
        compiler_params=params(),
        cost_estimate=pl.CostEstimate(flops=8_000_000, bytes_accessed=8_000_000, transcendentals=0),
        name="place_own",
    )(*pieces, key)
    weights, adopted, kept = pl.pallas_call(
        place_other_kernel,
        in_specs=[vmem] * 5 + [hbm] + [vmem] * 3,
        out_specs=[hbm] * 3,
        out_shape=[shape((256, 8192), BF), shape((3, 2, 8192), F32), shape((3, 2, 8192), F32)],
        scratch_shapes=[pltpu.VMEM((3, 2, 8192), F32)] * 2 + scratch + [pltpu.SemaphoreType.DMA((2,))],
        input_output_aliases={5: 0},
        compiler_params=params(),
        name="place_other",
    )(*other_pieces, key, weights, adopted, own_new, other_new)
    return (weights, kept.transpose(1, 0, 2), adopted.transpose(1, 0, 2)[None, None])


def solution(mesh):
    fine = Mesh(mesh.devices.reshape(4, 4, 4, 2), ("y", "z", "x", "core"))
    every = ("y", "z", "x", "core")
    in_specs = (P("y", ("z", "x", "core"), None, None), P(every, None), P(every, None), P(every, None), P())
    out_specs = (P(), P(every, None, None), P("y", ("z", "x", "core"), None, None, None))
    return jax.shard_map(body, mesh=fine, in_specs=in_specs, out_specs=out_specs, check_vma=False)
```

```python
import jax
import jax.numpy as jnp
from jax import lax
from jax.experimental import pallas as pl
from jax.experimental.pallas import tpu as pltpu
from jax.sharding import Mesh
from jax.sharding import PartitionSpec as P

ADAM_STEP = 20

beta_one = 0.9
beta_two = 0.95
learn_rate = 0.05
epsilon = 1e-08

CHIPS = ("y", "z", "x")
BF = jnp.bfloat16
F32 = jnp.float32
HALF = 4096


def adam_update(master, first, second, gradient):
    first_new = beta_one * first + (1.0 - beta_one) * gradient
    second_new = beta_two * second + (1.0 - beta_two) * gradient * gradient
    corr_one = 1.0 - beta_one**ADAM_STEP
    corr_two = 1.0 - beta_two**ADAM_STEP
    master_new = master - learn_rate * (first_new / corr_one) / (
        jnp.sqrt(second_new / corr_two) + epsilon
    )
    return (master_new, first_new, second_new)


def iota(shape, dim):
    return lax.broadcasted_iota(jnp.int32, shape, dim)


def one_hot(target):
    return jnp.where(iota(target.shape, 1) == target, 1.0, 0.0).astype(BF)


def pick(matrix, values):
    return jnp.dot(matrix, values, preferred_element_type=F32)


def columns(core):
    return pl.ds(pl.multiple_of(core * HALF, HALF), HALF)


def turned(rows):
    return pltpu.roll(rows, 4, axis=0)


def stack_kernel(master_ref, first_ref, out_ref):
    out_ref[0:2, :] = master_ref[...]
    out_ref[2:4, :] = first_ref[...]


def pair_kernel(master_ref, first_ref, second_ref, passed_ref, pair_ref):
    other = columns(1 - lax.axis_index("core"))
    pair_ref[...] = jnp.zeros_like(pair_ref)
    for i, ref in enumerate((master_ref, first_ref, second_ref)):
        pair_ref[2 * i : 2 * i + 2, :] = ref[:, other]
    pair_ref[8:12, :] = passed_ref[:, other]


def chip_class(chip):
    return (chip & 1) ^ (((chip >> 4) & 1) * 2) ^ (((chip >> 2) & 1) * 3)


def own_chip():
    return (lax.axis_index("y") * 4 + lax.axis_index("z")) * 4 + lax.axis_index("x")


def quarter(number):
    return pl.ds(pl.multiple_of(number * 256, 256), 256)


def add_kernel(
    grads_ref, got_ref, passed_ref, keep_ref, x_ref, y_ref, z_ref
):
    core = lax.axis_index("core")
    kind = chip_class(own_chip())
    low = iota((8, 256), 0) < 4
    pieces = (keep_ref, x_ref, y_ref, z_ref)

    def kept(i, carry):
        rows = pl.ds(pl.multiple_of(16 * i, 16), 16)
        for axis, ref in enumerate(pieces):
            parts = []
            for k in range(4):
                at = (kind ^ axis) * 4 + k
                parts.append(grads_ref[rows, quarter(core * 16 + at)].astype(F32) + got_ref[rows, quarter(at)].astype(F32))
            for tile in range(2):
                c = [part[8 * tile : 8 * tile + 8] for part in parts]
                even = [jnp.where(low, c[k], turned(c[k + 1])) for k in (0, 2)]
                odd = [jnp.where(low, turned(c[k]), c[k + 1]) for k in (0, 2)]
                for chip, block in ((4 * i + 2 * tile, even), (4 * i + 2 * tile + 1, odd)):
                    ref[chip] = jnp.concatenate(block, axis=0).astype(BF)
        return carry

    lax.fori_loop(0, 12, kept, 0)

    def leave(q, carry):
        for axis, ref in enumerate(pieces):
            rows = pl.ds(pl.multiple_of(192 + 16 * (kind ^ axis), 16), 16)
            total = grads_ref[rows, quarter(core * 16 + q)].astype(F32) + got_ref[rows, quarter(q)].astype(F32)
            ref[48 + q] = total.astype(BF)
        return carry

    lax.fori_loop(0, 16, leave, 0, unroll=4)


def merge_kernel(
    keep_ref, x_ref, y_ref, z_ref,
    master_ref, first_ref, second_ref, passed_ref, pair_ref, out_ref, old_ref, split_ref,
):
    core = lax.axis_index("core")

    def add(d, carry):
        total = keep_ref[d].astype(F32)
        for ref in (x_ref, y_ref, z_ref):
            total = total + ref[d].astype(F32)
        out_ref[d, :, 0:256] = total.astype(BF)
        return carry

    lax.fori_loop(0, 64, add, 0, unroll=8)

    old_ref[12:16, :] = jnp.zeros((4, HALF), F32)
    for mine in range(2):

        @pl.when(core == mine)
        def _():
            for i, ref in enumerate((master_ref, first_ref, second_ref)):
                at = 4 * i + 2 * mine
                old_ref[at : at + 2, :] = ref[:, mine * HALF : (mine + 1) * HALF]
                at = 4 * i + 2 * (1 - mine)
                old_ref[at : at + 2, :] = pair_ref[2 * i : 2 * i + 2, :]

    passed = passed_ref[:, columns(core)] + pair_ref[8:12, :]
    passed = jnp.where(lax.axis_index("y") == 3, old_ref[8:12, :], passed)
    high = passed.astype(BF).astype(F32)
    split_ref[0:4, :] = high
    split_ref[4:8, :] = passed - high

    def empty(d, carry):
        out_ref[d, :, 256:384] = jnp.zeros((16, 128), BF)
        return carry

    lax.fori_loop(0, 48, empty, 0, unroll=8)

    def leave(q, carry):
        parts = split_ref[:, quarter(q)]
        out_ref[48 + q, :, 256:384] = jnp.concatenate([parts[:, 0:128], parts[:, 128:256]], axis=0).astype(BF)
        return carry

    lax.fori_loop(0, 16, leave, 0, unroll=4)


def adam_kernel(parts_ref, chip_ref, owner_ref, out_ref, own_ref, other_ref, key_ref, old_ref):
    leaving = lax.axis_index("y") == 3
    core = lax.axis_index("core")
    totals = [jnp.zeros((16, 256), F32)] * 4
    for chip in range(64):
        kind = chip_class(chip)
        totals[kind] = totals[kind] + parts_ref[chip, :, 0:256].astype(F32)
    gradient = jnp.concatenate(totals, axis=1)

    @pl.when(leaving)
    def _():
        for y in (0, 2, 3):
            for q in range(16):
                parts = parts_ref[16 * y + q, :, 256:384].astype(F32)
                row = 4 * (q % 4)
                for h in range(2):
                    value = parts[8 * h : 8 * h + 4] + parts[8 * h + 4 : 8 * h + 8]
                    cut = slice((q // 4) * 256 + h * 128, (q // 4) * 256 + h * 128 + 128)
                    if y == 3:
                        old_ref[2, row : row + 4, cut] = value
                    else:
                        old_ref[0, row + y : row + y + 2, cut] = value[0:2]
                        old_ref[1, row + y : row + y + 2, cut] = value[2:4]

    @pl.when(jnp.logical_not(leaving))
    def _():
        for i in range(3):
            for n in range(16):
                k, u = n % 4, n // 4
                old_ref[i, 4 * k : 4 * k + 4, u * 256 : (u + 1) * 256] = chip_ref[
                    4 * i : 4 * i + 4, n * 256 : (n + 1) * 256
                ]

    new = adam_update(old_ref[0], old_ref[1], old_ref[2], gradient)
    own_ref[6:8, :] = jnp.zeros((2, HALF), F32)
    other_ref[6:8, :] = jnp.zeros((2, HALF), F32)
    values = [jnp.where(leaving, jnp.zeros_like(value), value) for value in new]
    for mine in range(2):

        @pl.when(core == mine)
        def _():
            for i in range(3):
                for n in range(16):
                    k, u = n % 4, n // 4
                    cut, lanes = slice(n * 256, (n + 1) * 256), slice(u * 256, (u + 1) * 256)
                    at = 4 * k + 2 * mine
                    own_ref[2 * i : 2 * i + 2, cut] = values[i][at : at + 2, lanes]
                    at = 4 * k + 2 * (1 - mine)
                    other_ref[2 * i : 2 * i + 2, cut] = values[i][at : at + 2, lanes]

    weights = new[0].astype(BF)

    for chip in range(64):
        kind = chip_class(chip)
        out_ref[chip, :, 0:256] = weights[:, kind * 256 : (kind + 1) * 256]

    lane, row = iota((64, 256), 1), iota((64, 256), 0)
    tiled = jnp.where((lane & 63) == row, 1.0, 0.0).astype(BF)
    across = pick(jnp.broadcast_to(owner_ref[...], (64, 64)).astype(F32).astype(BF), tiled)
    down = jnp.sum(jnp.where(lane == row, across, 0.0), axis=1, keepdims=True)
    earlier = (across == down) & (row < (lane & 63))
    slot = jnp.sum(jnp.where(earlier, 1.0, 0.0), axis=0, keepdims=True)
    key = (across[0:1, :] * 2.0 + slot).astype(jnp.int32) + 512 * (iota((1, 256), 1) >> 6)
    key_ref[...] = key
    moments = jnp.concatenate(
        [
            new[1 + part // 2][:, a * 256 + (part % 2) * 128 : a * 256 + (part % 2) * 128 + 128]
            for part in range(4)
            for a in range(4)
        ],
        axis=0,
    ).astype(BF)
    p = iota((1024, 256), 0)
    wanted = (p >> 4) * 4 + (p & 3) + 512 * ((p >> 2) & 3)
    chosen = jnp.where(key == wanted, 1.0, 0.0).astype(BF)
    out_ref[:, :, 256:384] = pick(chosen, moments).astype(BF).reshape(64, 16, 128)


def copy_kernel(blocks_ref, out_ref):
    out_ref[...] = blocks_ref[:, :, 0:256]


def place_half(views, key_ref, weights_ref, adopted_ref, adopted_at, adopted_ready, rows_ref, sems, core, side):
    blocks_ref = views[0][0]
    chip = own_chip()
    kind = chip_class(chip)
    low = iota((8, 256), 0) < 4

    def store(i):
        rows = pl.ds(pl.multiple_of(32 * i, 32), 32)
        return pltpu.make_async_copy(rows_ref.at[rows, :], weights_ref.at[rows, columns(side)], sems.at[i])

    def kept(i, carry):
        for axis in range(4):
            ref, lane = views[axis]
            for g in range(2):
                tiles = []
                for tile in range(2):
                    number = 8 * i + 4 * g + 2 * tile
                    even = ref[number, :, lane : lane + 256].astype(F32)
                    odd = ref[number + 1, :, lane : lane + 256].astype(F32)
                    cut = []
                    for s in (slice(0, 8), slice(8, 16)):
                        cut.append(jnp.where(low, even[s], turned(odd[s])))
                        cut.append(jnp.where(low, turned(even[s]), odd[s]))
                    tiles.append(cut)
                rows = pl.ds(pl.multiple_of(32 * i + 16 * g, 16), 16)
                for k in range(4):
                    rows_ref[rows, quarter((kind ^ axis) * 4 + k)] = jnp.concatenate(
                        [tiles[0][k], tiles[1][k]], axis=0
                    ).astype(BF)
        store(i).start()
        return carry

    for axis in range(4):
        ref, lane = views[axis]
        rows = pl.ds(pl.multiple_of(192 + 16 * (kind ^ axis), 16), 16)
        for q in range(16):
            rows_ref[rows, q * 256 : (q + 1) * 256] = ref[48 + q, :, lane : lane + 256]
    for i in range(6, 8):
        store(i).start()
    k = iota((8, 64), 0)
    wanted = jnp.where(k < 2, chip * 4 + core * 2 + k, -1)
    chosen = jnp.where(key_ref[:, 0:64] == wanted, 1.0, 0.0).astype(BF)
    masters = pick(chosen, rows_ref[192:256, :])
    adopted_ref[0, :, adopted_at(0, HALF)] = masters[0:2, :]
    moments = jnp.concatenate([blocks_ref[48 + q, :, 256:384] for q in range(16)], axis=1)
    for h in range(2):
        k = iota((8, 16), 0)
        found = pick(one_hot(jnp.where(k < 4, ((k >> 1) * 2 + h) * 4 + core * 2 + (k & 1), -1)), moments)
        for q in range(16):
            for i in range(2):
                adopted_ref[1 + i, :, adopted_at(q * 256 + h * 128, 128)] = found[
                    2 * i : 2 * i + 2, q * 128 : (q + 1) * 128
                ]
    adopted_ready()
    lax.fori_loop(0, 6, kept, 0)
    for i in range(8):
        store(i).wait()


def place_own_kernel(
    blocks_ref, x_ref, y_ref, z_ref, key_ref, weights_ref, adopted_ref, rows_ref, sems
):
    views = [(ref, 0) for ref in (blocks_ref, x_ref, y_ref, z_ref)]
    core = lax.axis_index("core")
    place_half(
        views, key_ref, weights_ref, adopted_ref, lambda start, size: slice(start, start + size), lambda: None,
        rows_ref, sems, core, core,
    )


def place_other_kernel(*refs):
    key_ref, _, half_ref, own_ref, other_ref = refs[4:9]
    weights_ref, adopted_out, kept_out, adopted_ref, kept_ref, rows_ref, sems, out_sems = refs[9:]
    views = [(ref, 0) for ref in refs[:4]]
    core = lax.axis_index("core")
    side = 1 - core
    kept_copy = pltpu.make_async_copy(kept_ref, kept_out, out_sems.at[0])
    adopted_copy = pltpu.make_async_copy(adopted_ref, adopted_out, out_sems.at[1])
    for i in range(3):
        adopted_ref[i, :, columns(core)] = half_ref[i]
        kept_ref[i, :, columns(core)] = own_ref[2 * i : 2 * i + 2, :]
        kept_ref[i, :, columns(side)] = other_ref[2 * i : 2 * i + 2, :]
    kept_copy.start()

    def at(start, size):
        return pl.ds(pl.multiple_of(side * HALF + start, 128), size)

    place_half(views, key_ref, weights_ref, adopted_ref, at, adopted_copy.start, rows_ref, sems, core, side)
    kept_copy.wait()
    adopted_copy.wait()


def params(mib=40):
    return pltpu.CompilerParams(vmem_limit_bytes=mib * 1024 * 1024)


def shape(dims, dtype):
    return jax.ShapeDtypeStruct(dims, dtype)


def swapped(value):
    return lax.ppermute(value, "core", [(0, 1), (1, 0)])


def to_neighbours(values):
    pairs = [(2 * p + c, 2 * ((p + 3 - 2 * c) % 4) + c) for p in range(4) for c in range(2)]
    return [lax.ppermute(value, (axis, "core"), pairs) for axis, value in zip("xyz", values)]


def from_leaving(value):
    pairs = [(96 + rank, 64 * (rank % 2) + rank) for rank in range(32)]
    return lax.ppermute(value, ("y", "z", "x", "core"), pairs)


def body(local_grads, master, first, second, new_owner):
    grads = local_grads.reshape(256, 8192)
    vmem = pl.BlockSpec(memory_space=pltpu.VMEM)
    hbm = pl.BlockSpec(memory_space=pltpu.HBM)
    core = lax.axis_index("core")
    got = swapped(lax.dynamic_slice(grads, (0, (1 - core) * HALF), (256, HALF)))
    stacked = pl.pallas_call(
        stack_kernel,
        in_specs=[vmem] * 2,
        out_specs=vmem,
        out_shape=shape((4, 8192), F32),
        compiler_params=params(),
        name="stack",
    )(master, first)
    passed = from_leaving(stacked)
    piece = shape((64, 16, 256), BF)
    keep, *to_send = pl.pallas_call(
        add_kernel,
        in_specs=[vmem] * 3,
        out_specs=[vmem] * 4,
        out_shape=[piece] * 4,
        compiler_params=params(),
        name="add_blocks",
    )(grads, got, passed)
    pair = pl.pallas_call(
        pair_kernel,
        in_specs=[vmem] * 4,
        out_specs=vmem,
        out_shape=shape((16, HALF), F32),
        compiler_params=params(),
        name="pair",
    )(master, first, second, passed)
    arrived = to_neighbours(to_send)
    pair = swapped(pair)
    partial, old = pl.pallas_call(
        merge_kernel,
        in_specs=[vmem] * 9,
        out_specs=[vmem] * 2,
        out_shape=[shape((64, 16, 384), BF), shape((16, HALF), F32)],
        scratch_shapes=[pltpu.VMEM((8, HALF), F32)],
        compiler_params=params(),
        name="merge",
    )(keep, *arrived, master, first, second, passed, pair)
    partial = lax.all_to_all(partial, CHIPS, 0, 0, tiled=True)
    payload, own_new, other_new, key = pl.pallas_call(
        adam_kernel,
        in_specs=[vmem] * 3,
        out_specs=[vmem] * 4,
        out_shape=[
            shape((64, 16, 384), BF),
            shape((8, HALF), F32),
            shape((8, HALF), F32),
            shape((1, 256), jnp.int32),
        ],
        scratch_shapes=[pltpu.VMEM((3, 16, 1024), F32)],
        compiler_params=params(),
        name="adam",
    )(partial, old, new_owner.reshape(1, 64))
    other_new = swapped(other_new)
    blocks = lax.all_to_all(payload, CHIPS, 0, 0, tiled=True)
    mine = pl.pallas_call(
        copy_kernel,
        in_specs=[vmem],
        out_specs=vmem,
        out_shape=piece,
        compiler_params=params(),
        name="mine",
    )(blocks)
    pieces = [blocks] + to_neighbours([mine] * 3)
    other_pieces = [swapped(value) for value in pieces]
    scratch = [pltpu.VMEM((256, HALF), BF), pltpu.SemaphoreType.DMA((8,))]
    weights, adopted = pl.pallas_call(
        place_own_kernel,
        in_specs=[vmem] * 5,
        out_specs=[hbm, vmem],
        out_shape=[shape((256, 8192), BF), shape((3, 2, HALF), F32)],
        scratch_shapes=scratch,
        compiler_params=params(),
        cost_estimate=pl.CostEstimate(flops=8_000_000, bytes_accessed=8_000_000, transcendentals=0),
        name="place_own",
    )(*pieces, key)
    weights, adopted, kept = pl.pallas_call(
        place_other_kernel,
        in_specs=[vmem] * 5 + [hbm] + [vmem] * 3,
        out_specs=[hbm] * 3,
        out_shape=[shape((256, 8192), BF), shape((3, 2, 8192), F32), shape((3, 2, 8192), F32)],
        scratch_shapes=[pltpu.VMEM((3, 2, 8192), F32)] * 2 + scratch + [pltpu.SemaphoreType.DMA((2,))],
        input_output_aliases={5: 0},
        compiler_params=params(),
        name="place_other",
    )(*other_pieces, key, weights, adopted, own_new, other_new)
    return (weights, kept.transpose(1, 0, 2), adopted.transpose(1, 0, 2)[None, None])


def solution(mesh):
    fine = Mesh(mesh.devices.reshape(4, 4, 4, 2), ("y", "z", "x", "core"))
    every = ("y", "z", "x", "core")
    in_specs = (P("y", ("z", "x", "core"), None, None), P(every, None), P(every, None), P(every, None), P())
    out_specs = (P(), P(every, None, None), P("y", ("z", "x", "core"), None, None, None))
    return jax.shard_map(body, mesh=fine, in_specs=in_specs, out_specs=out_specs, check_vma=False)
```

```python
import jax
import jax.numpy as jnp
from jax import lax
from jax.experimental import pallas as pl
from jax.experimental.pallas import tpu as pltpu
from jax.sharding import Mesh
from jax.sharding import PartitionSpec as P

ADAM_STEP = 20

beta_one = 0.9
beta_two = 0.95
learn_rate = 0.05
epsilon = 1e-08

CHIPS = ("y", "z", "x")
BF = jnp.bfloat16
F32 = jnp.float32
HALF = 4096


def adam_update(master, first, second, gradient):
    first_new = beta_one * first + (1.0 - beta_one) * gradient
    second_new = beta_two * second + (1.0 - beta_two) * gradient * gradient
    corr_one = 1.0 - beta_one**ADAM_STEP
    corr_two = 1.0 - beta_two**ADAM_STEP
    master_new = master - learn_rate * (first_new / corr_one) / (
        jnp.sqrt(second_new / corr_two) + epsilon
    )
    return (master_new, first_new, second_new)


def iota(shape, dim):
    return lax.broadcasted_iota(jnp.int32, shape, dim)


def one_hot(target):
    return jnp.where(iota(target.shape, 1) == target, 1.0, 0.0).astype(BF)


def pick(matrix, values):
    return jnp.dot(matrix, values, preferred_element_type=F32)


def columns(core):
    return pl.ds(pl.multiple_of(core * HALF, HALF), HALF)


def turned(rows):
    return pltpu.roll(rows, 4, axis=0)


def stack_kernel(master_ref, first_ref, out_ref):
    out_ref[0:2, :] = master_ref[...]
    out_ref[2:4, :] = first_ref[...]


def pair_kernel(master_ref, first_ref, second_ref, passed_ref, pair_ref):
    other = columns(1 - lax.axis_index("core"))
    pair_ref[...] = jnp.zeros_like(pair_ref)
    for i, ref in enumerate((master_ref, first_ref, second_ref)):
        pair_ref[2 * i : 2 * i + 2, :] = ref[:, other]
    pair_ref[8:12, :] = passed_ref[:, other]


def chip_class(chip):
    return (chip & 1) ^ (((chip >> 4) & 1) * 2) ^ (((chip >> 2) & 1) * 3)


def own_chip():
    return (lax.axis_index("y") * 4 + lax.axis_index("z")) * 4 + lax.axis_index("x")


def quarter(number):
    return pl.ds(pl.multiple_of(number * 256, 256), 256)


def add_kernel(
    grads_ref, got_ref, passed_ref, keep_ref, x_ref, y_ref, z_ref
):
    core = lax.axis_index("core")
    kind = chip_class(own_chip())
    low = iota((8, 256), 0) < 4
    pieces = (keep_ref, x_ref, y_ref, z_ref)

    def kept(i, carry):
        rows = pl.ds(pl.multiple_of(16 * i, 16), 16)
        for axis, ref in enumerate(pieces):
            parts = []
            for k in range(4):
                at = (kind ^ axis) * 4 + k
                parts.append(grads_ref[rows, quarter(core * 16 + at)].astype(F32) + got_ref[rows, quarter(at)].astype(F32))
            for tile in range(2):
                c = [part[8 * tile : 8 * tile + 8] for part in parts]
                even = [jnp.where(low, c[k], turned(c[k + 1])) for k in (0, 2)]
                odd = [jnp.where(low, turned(c[k]), c[k + 1]) for k in (0, 2)]
                for chip, block in ((4 * i + 2 * tile, even), (4 * i + 2 * tile + 1, odd)):
                    ref[chip] = jnp.concatenate(block, axis=0).astype(BF)
        return carry

    lax.fori_loop(0, 12, kept, 0, unroll=6)

    def leave(q, carry):
        for axis, ref in enumerate(pieces):
            rows = pl.ds(pl.multiple_of(192 + 16 * (kind ^ axis), 16), 16)
            total = grads_ref[rows, quarter(core * 16 + q)].astype(F32) + got_ref[rows, quarter(q)].astype(F32)
            ref[48 + q] = total.astype(BF)
        return carry

    lax.fori_loop(0, 16, leave, 0, unroll=16)


def merge_kernel(
    keep_ref, x_ref, y_ref, z_ref,
    master_ref, first_ref, second_ref, passed_ref, pair_ref, out_ref, old_ref, split_ref,
):
    core = lax.axis_index("core")

    def add(d, carry):
        total = keep_ref[d].astype(F32)
        for ref in (x_ref, y_ref, z_ref):
            total = total + ref[d].astype(F32)
        out_ref[d, :, 0:256] = total.astype(BF)
        return carry

    lax.fori_loop(0, 64, add, 0, unroll=16)

    old_ref[12:16, :] = jnp.zeros((4, HALF), F32)
    for mine in range(2):

        @pl.when(core == mine)
        def _():
            for i, ref in enumerate((master_ref, first_ref, second_ref)):
                at = 4 * i + 2 * mine
                old_ref[at : at + 2, :] = ref[:, mine * HALF : (mine + 1) * HALF]
                at = 4 * i + 2 * (1 - mine)
                old_ref[at : at + 2, :] = pair_ref[2 * i : 2 * i + 2, :]

    passed = passed_ref[:, columns(core)] + pair_ref[8:12, :]
    passed = jnp.where(lax.axis_index("y") == 3, old_ref[8:12, :], passed)
    high = passed.astype(BF).astype(F32)
    split_ref[0:4, :] = high
    split_ref[4:8, :] = passed - high

    def empty(d, carry):
        out_ref[d, :, 256:384] = jnp.zeros((16, 128), BF)
        return carry

    lax.fori_loop(0, 48, empty, 0, unroll=8)

    def leave(q, carry):
        parts = split_ref[:, quarter(q)]
        out_ref[48 + q, :, 256:384] = jnp.concatenate([parts[:, 0:128], parts[:, 128:256]], axis=0).astype(BF)
        return carry

    lax.fori_loop(0, 16, leave, 0, unroll=16)


def adam_kernel(parts_ref, chip_ref, owner_ref, out_ref, own_ref, other_ref, key_ref, old_ref):
    leaving = lax.axis_index("y") == 3
    core = lax.axis_index("core")
    totals = [jnp.zeros((16, 256), F32)] * 4
    for chip in range(64):
        kind = chip_class(chip)
        totals[kind] = totals[kind] + parts_ref[chip, :, 0:256].astype(F32)
    gradient = jnp.concatenate(totals, axis=1)

    @pl.when(leaving)
    def _():
        for y in (0, 2, 3):
            for q in range(16):
                parts = parts_ref[16 * y + q, :, 256:384].astype(F32)
                row = 4 * (q % 4)
                for h in range(2):
                    value = parts[8 * h : 8 * h + 4] + parts[8 * h + 4 : 8 * h + 8]
                    cut = slice((q // 4) * 256 + h * 128, (q // 4) * 256 + h * 128 + 128)
                    if y == 3:
                        old_ref[2, row : row + 4, cut] = value
                    else:
                        old_ref[0, row + y : row + y + 2, cut] = value[0:2]
                        old_ref[1, row + y : row + y + 2, cut] = value[2:4]

    @pl.when(jnp.logical_not(leaving))
    def _():
        for i in range(3):
            for n in range(16):
                k, u = n % 4, n // 4
                old_ref[i, 4 * k : 4 * k + 4, u * 256 : (u + 1) * 256] = chip_ref[
                    4 * i : 4 * i + 4, n * 256 : (n + 1) * 256
                ]

    new = adam_update(old_ref[0], old_ref[1], old_ref[2], gradient)
    own_ref[6:8, :] = jnp.zeros((2, HALF), F32)
    other_ref[6:8, :] = jnp.zeros((2, HALF), F32)
    values = [jnp.where(leaving, jnp.zeros_like(value), value) for value in new]
    for mine in range(2):

        @pl.when(core == mine)
        def _():
            for i in range(3):
                for n in range(16):
                    k, u = n % 4, n // 4
                    cut, lanes = slice(n * 256, (n + 1) * 256), slice(u * 256, (u + 1) * 256)
                    at = 4 * k + 2 * mine
                    own_ref[2 * i : 2 * i + 2, cut] = values[i][at : at + 2, lanes]
                    at = 4 * k + 2 * (1 - mine)
                    other_ref[2 * i : 2 * i + 2, cut] = values[i][at : at + 2, lanes]

    weights = new[0].astype(BF)

    for chip in range(64):
        kind = chip_class(chip)
        out_ref[chip, :, 0:256] = weights[:, kind * 256 : (kind + 1) * 256]

    lane, row = iota((64, 256), 1), iota((64, 256), 0)
    tiled = jnp.where((lane & 63) == row, 1.0, 0.0).astype(BF)
    across = pick(jnp.broadcast_to(owner_ref[...], (64, 64)).astype(F32).astype(BF), tiled)
    down = jnp.sum(jnp.where(lane == row, across, 0.0), axis=1, keepdims=True)
    earlier = (across == down) & (row < (lane & 63))
    slot = jnp.sum(jnp.where(earlier, 1.0, 0.0), axis=0, keepdims=True)
    key = (across[0:1, :] * 2.0 + slot).astype(jnp.int32) + 512 * (iota((1, 256), 1) >> 6)
    key_ref[...] = key
    moments = jnp.concatenate(
        [
            new[1 + part // 2][:, a * 256 + (part % 2) * 128 : a * 256 + (part % 2) * 128 + 128]
            for part in range(4)
            for a in range(4)
        ],
        axis=0,
    ).astype(BF)
    p = iota((1024, 256), 0)
    wanted = (p >> 4) * 4 + (p & 3) + 512 * ((p >> 2) & 3)
    chosen = jnp.where(key == wanted, 1.0, 0.0).astype(BF)
    out_ref[:, :, 256:384] = pick(chosen, moments).astype(BF).reshape(64, 16, 128)


def copy_kernel(blocks_ref, out_ref):
    out_ref[...] = blocks_ref[:, :, 0:256]


def place_half(views, key_ref, weights_ref, adopted_ref, adopted_at, adopted_ready, rows_ref, sems, core, side):
    blocks_ref = views[0][0]
    chip = own_chip()
    kind = chip_class(chip)
    low = iota((8, 256), 0) < 4

    def store(i):
        rows = pl.ds(pl.multiple_of(32 * i, 32), 32)
        return pltpu.make_async_copy(rows_ref.at[rows, :], weights_ref.at[rows, columns(side)], sems.at[i])

    def kept(i, carry):
        for axis in range(4):
            ref, lane = views[axis]
            for g in range(2):
                tiles = []
                for tile in range(2):
                    number = 8 * i + 4 * g + 2 * tile
                    even = ref[number, :, lane : lane + 256].astype(F32)
                    odd = ref[number + 1, :, lane : lane + 256].astype(F32)
                    cut = []
                    for s in (slice(0, 8), slice(8, 16)):
                        cut.append(jnp.where(low, even[s], turned(odd[s])))
                        cut.append(jnp.where(low, turned(even[s]), odd[s]))
                    tiles.append(cut)
                rows = pl.ds(pl.multiple_of(32 * i + 16 * g, 16), 16)
                for k in range(4):
                    rows_ref[rows, quarter((kind ^ axis) * 4 + k)] = jnp.concatenate(
                        [tiles[0][k], tiles[1][k]], axis=0
                    ).astype(BF)
        store(i).start()
        return carry

    for axis in range(4):
        ref, lane = views[axis]
        rows = pl.ds(pl.multiple_of(192 + 16 * (kind ^ axis), 16), 16)
        for q in range(16):
            rows_ref[rows, q * 256 : (q + 1) * 256] = ref[48 + q, :, lane : lane + 256]
    for i in range(6, 8):
        store(i).start()
    k = iota((8, 64), 0)
    wanted = jnp.where(k < 2, chip * 4 + core * 2 + k, -1)
    chosen = jnp.where(key_ref[:, 0:64] == wanted, 1.0, 0.0).astype(BF)
    masters = pick(chosen, rows_ref[192:256, :])
    adopted_ref[0, :, adopted_at(0, HALF)] = masters[0:2, :]
    moments = jnp.concatenate([blocks_ref[48 + q, :, 256:384] for q in range(16)], axis=1)
    for h in range(2):
        k = iota((8, 16), 0)
        found = pick(one_hot(jnp.where(k < 4, ((k >> 1) * 2 + h) * 4 + core * 2 + (k & 1), -1)), moments)
        for q in range(16):
            for i in range(2):
                adopted_ref[1 + i, :, adopted_at(q * 256 + h * 128, 128)] = found[
                    2 * i : 2 * i + 2, q * 128 : (q + 1) * 128
                ]
    adopted_ready()
    lax.fori_loop(0, 6, kept, 0, unroll=6)
    for i in range(8):
        store(i).wait()


def place_own_kernel(
    blocks_ref, x_ref, y_ref, z_ref, key_ref, weights_ref, adopted_ref, rows_ref, sems
):
    views = [(ref, 0) for ref in (blocks_ref, x_ref, y_ref, z_ref)]
    core = lax.axis_index("core")
    place_half(
        views, key_ref, weights_ref, adopted_ref, lambda start, size: slice(start, start + size), lambda: None,
        rows_ref, sems, core, core,
    )


def place_other_kernel(*refs):
    key_ref, _, half_ref, own_ref, other_ref = refs[4:9]
    weights_ref, adopted_out, kept_out, adopted_ref, kept_ref, rows_ref, sems, out_sems = refs[9:]
    views = [(ref, 0) for ref in refs[:4]]
    core = lax.axis_index("core")
    side = 1 - core
    kept_copy = pltpu.make_async_copy(kept_ref, kept_out, out_sems.at[0])
    adopted_copy = pltpu.make_async_copy(adopted_ref, adopted_out, out_sems.at[1])
    for i in range(3):
        adopted_ref[i, :, columns(core)] = half_ref[i]
        kept_ref[i, :, columns(core)] = own_ref[2 * i : 2 * i + 2, :]
        kept_ref[i, :, columns(side)] = other_ref[2 * i : 2 * i + 2, :]
    kept_copy.start()

    def at(start, size):
        return pl.ds(pl.multiple_of(side * HALF + start, 128), size)

    place_half(views, key_ref, weights_ref, adopted_ref, at, adopted_copy.start, rows_ref, sems, core, side)
    kept_copy.wait()
    adopted_copy.wait()


def params(mib=40):
    return pltpu.CompilerParams(vmem_limit_bytes=mib * 1024 * 1024)


def shape(dims, dtype):
    return jax.ShapeDtypeStruct(dims, dtype)


def swapped(value):
    return lax.ppermute(value, "core", [(0, 1), (1, 0)])


def to_neighbours(values):
    pairs = [(2 * p + c, 2 * ((p + 3 - 2 * c) % 4) + c) for p in range(4) for c in range(2)]
    return [lax.ppermute(value, (axis, "core"), pairs) for axis, value in zip("xyz", values)]


def from_leaving(value):
    pairs = [(96 + rank, 64 * (rank % 2) + rank) for rank in range(32)]
    return lax.ppermute(value, ("y", "z", "x", "core"), pairs)


def body(local_grads, master, first, second, new_owner):
    grads = local_grads.reshape(256, 8192)
    vmem = pl.BlockSpec(memory_space=pltpu.VMEM)
    hbm = pl.BlockSpec(memory_space=pltpu.HBM)
    core = lax.axis_index("core")
    got = swapped(lax.dynamic_slice(grads, (0, (1 - core) * HALF), (256, HALF)))
    stacked = pl.pallas_call(
        stack_kernel,
        in_specs=[vmem] * 2,
        out_specs=vmem,
        out_shape=shape((4, 8192), F32),
        compiler_params=params(),
        name="stack",
    )(master, first)
    passed = from_leaving(stacked)
    piece = shape((64, 16, 256), BF)
    keep, *to_send = pl.pallas_call(
        add_kernel,
        in_specs=[vmem] * 3,
        out_specs=[vmem] * 4,
        out_shape=[piece] * 4,
        compiler_params=params(),
        name="add_blocks",
    )(grads, got, passed)
    pair = pl.pallas_call(
        pair_kernel,
        in_specs=[vmem] * 4,
        out_specs=vmem,
        out_shape=shape((16, HALF), F32),
        compiler_params=params(),
        name="pair",
    )(master, first, second, passed)
    arrived = to_neighbours(to_send)
    pair = swapped(pair)
    partial, old = pl.pallas_call(
        merge_kernel,
        in_specs=[vmem] * 9,
        out_specs=[vmem] * 2,
        out_shape=[shape((64, 16, 384), BF), shape((16, HALF), F32)],
        scratch_shapes=[pltpu.VMEM((8, HALF), F32)],
        compiler_params=params(),
        name="merge",
    )(keep, *arrived, master, first, second, passed, pair)
    partial = lax.all_to_all(partial, CHIPS, 0, 0, tiled=True)
    payload, own_new, other_new, key = pl.pallas_call(
        adam_kernel,
        in_specs=[vmem] * 3,
        out_specs=[vmem] * 4,
        out_shape=[
            shape((64, 16, 384), BF),
            shape((8, HALF), F32),
            shape((8, HALF), F32),
            shape((1, 256), jnp.int32),
        ],
        scratch_shapes=[pltpu.VMEM((3, 16, 1024), F32)],
        compiler_params=params(),
        name="adam",
    )(partial, old, new_owner.reshape(1, 64))
    other_new = swapped(other_new)
    blocks = lax.all_to_all(payload, CHIPS, 0, 0, tiled=True)
    mine = pl.pallas_call(
        copy_kernel,
        in_specs=[vmem],
        out_specs=vmem,
        out_shape=piece,
        compiler_params=params(),
        name="mine",
    )(blocks)
    pieces = [blocks] + to_neighbours([mine] * 3)
    other_pieces = [swapped(value) for value in pieces]
    scratch = [pltpu.VMEM((256, HALF), BF), pltpu.SemaphoreType.DMA((8,))]
    weights, adopted = pl.pallas_call(
        place_own_kernel,
        in_specs=[vmem] * 5,
        out_specs=[hbm, vmem],
        out_shape=[shape((256, 8192), BF), shape((3, 2, HALF), F32)],
        scratch_shapes=scratch,
        compiler_params=params(),
        cost_estimate=pl.CostEstimate(flops=8_000_000, bytes_accessed=8_000_000, transcendentals=0),
        name="place_own",
    )(*pieces, key)
    weights, adopted, kept = pl.pallas_call(
        place_other_kernel,
        in_specs=[vmem] * 5 + [hbm] + [vmem] * 3,
        out_specs=[hbm] * 3,
        out_shape=[shape((256, 8192), BF), shape((3, 2, 8192), F32), shape((3, 2, 8192), F32)],
        scratch_shapes=[pltpu.VMEM((3, 2, 8192), F32)] * 2 + scratch + [pltpu.SemaphoreType.DMA((2,))],
        input_output_aliases={5: 0},
        compiler_params=params(),
        name="place_other",
    )(*other_pieces, key, weights, adopted, own_new, other_new)
    return (weights, kept.transpose(1, 0, 2), adopted.transpose(1, 0, 2)[None, None])


def solution(mesh):
    fine = Mesh(mesh.devices.reshape(4, 4, 4, 2), ("y", "z", "x", "core"))
    every = ("y", "z", "x", "core")
    in_specs = (P("y", ("z", "x", "core"), None, None), P(every, None), P(every, None), P(every, None), P())
    out_specs = (P(), P(every, None, None), P("y", ("z", "x", "core"), None, None, None))
    return jax.shard_map(body, mesh=fine, in_specs=in_specs, out_specs=out_specs, check_vma=False)
```

```python
import jax
import jax.numpy as jnp
from jax import lax
from jax.experimental import pallas as pl
from jax.experimental.pallas import tpu as pltpu
from jax.sharding import Mesh
from jax.sharding import PartitionSpec as P

ADAM_STEP = 20

beta_one = 0.9
beta_two = 0.95
learn_rate = 0.05
epsilon = 1e-08

CHIPS = ("y", "z", "x")
BF = jnp.bfloat16
F32 = jnp.float32
HALF = 4096


def adam_update(master, first, second, gradient):
    first_new = beta_one * first + (1.0 - beta_one) * gradient
    second_new = beta_two * second + (1.0 - beta_two) * gradient * gradient
    corr_one = 1.0 - beta_one**ADAM_STEP
    corr_two = 1.0 - beta_two**ADAM_STEP
    master_new = master - learn_rate * (first_new / corr_one) / (
        jnp.sqrt(second_new / corr_two) + epsilon
    )
    return (master_new, first_new, second_new)


def iota(shape, dim):
    return lax.broadcasted_iota(jnp.int32, shape, dim)


def one_hot(target):
    return jnp.where(iota(target.shape, 1) == target, 1.0, 0.0).astype(BF)


def pick(matrix, values):
    return jnp.dot(matrix, values, preferred_element_type=F32)


def columns(core):
    return pl.ds(pl.multiple_of(core * HALF, HALF), HALF)


def turned(rows):
    return pltpu.roll(rows, 4, axis=0)


def stack_kernel(master_ref, first_ref, out_ref):
    out_ref[0:2, :] = master_ref[...]
    out_ref[2:4, :] = first_ref[...]


def pair_kernel(master_ref, first_ref, second_ref, passed_ref, pair_ref):
    other = columns(1 - lax.axis_index("core"))
    pair_ref[6:8, :] = jnp.zeros((2, HALF), F32)
    for i, ref in enumerate((master_ref, first_ref, second_ref)):
        pair_ref[2 * i : 2 * i + 2, :] = ref[:, other]
    pair_ref[8:12, :] = passed_ref[:, other]


def chip_class(chip):
    return (chip & 1) ^ (((chip >> 4) & 1) * 2) ^ (((chip >> 2) & 1) * 3)


def own_chip():
    return (lax.axis_index("y") * 4 + lax.axis_index("z")) * 4 + lax.axis_index("x")


def quarter(number):
    return pl.ds(pl.multiple_of(number * 256, 256), 256)


def add_kernel(
    grads_ref, got_ref, passed_ref, keep_ref, x_ref, y_ref, z_ref
):
    core = lax.axis_index("core")
    kind = chip_class(own_chip())
    low = iota((8, 256), 0) < 4
    pieces = (keep_ref, x_ref, y_ref, z_ref)

    def kept(i, carry):
        rows = pl.ds(pl.multiple_of(16 * i, 16), 16)
        for axis, ref in enumerate(pieces):
            parts = []
            for k in range(4):
                at = (kind ^ axis) * 4 + k
                parts.append(grads_ref[rows, quarter(core * 16 + at)].astype(F32) + got_ref[rows, quarter(at)].astype(F32))
            for tile in range(2):
                c = [part[8 * tile : 8 * tile + 8] for part in parts]
                even = [jnp.where(low, c[k], turned(c[k + 1])) for k in (0, 2)]
                odd = [jnp.where(low, turned(c[k]), c[k + 1]) for k in (0, 2)]
                for chip, block in ((4 * i + 2 * tile, even), (4 * i + 2 * tile + 1, odd)):
                    ref[chip] = jnp.concatenate(block, axis=0).astype(BF)
        return carry

    lax.fori_loop(0, 12, kept, 0, unroll=12)

    def leave(q, carry):
        for axis, ref in enumerate(pieces):
            rows = pl.ds(pl.multiple_of(192 + 16 * (kind ^ axis), 16), 16)
            total = grads_ref[rows, quarter(core * 16 + q)].astype(F32) + got_ref[rows, quarter(q)].astype(F32)
            ref[48 + q] = total.astype(BF)
        return carry

    lax.fori_loop(0, 16, leave, 0, unroll=16)


def merge_kernel(
    keep_ref, x_ref, y_ref, z_ref,
    master_ref, first_ref, second_ref, passed_ref, pair_ref, out_ref, old_ref, split_ref,
):
    core = lax.axis_index("core")

    def add(d, carry):
        total = keep_ref[d].astype(F32)
        for ref in (x_ref, y_ref, z_ref):
            total = total + ref[d].astype(F32)
        out_ref[d, :, 0:256] = total.astype(BF)
        return carry

    lax.fori_loop(0, 64, add, 0, unroll=64)

    old_ref[12:16, :] = jnp.zeros((4, HALF), F32)
    for mine in range(2):

        @pl.when(core == mine)
        def _():
            for i, ref in enumerate((master_ref, first_ref, second_ref)):
                at = 4 * i + 2 * mine
                old_ref[at : at + 2, :] = ref[:, mine * HALF : (mine + 1) * HALF]
                at = 4 * i + 2 * (1 - mine)
                old_ref[at : at + 2, :] = pair_ref[2 * i : 2 * i + 2, :]

    passed = passed_ref[:, columns(core)] + pair_ref[8:12, :]
    passed = jnp.where(lax.axis_index("y") == 3, old_ref[8:12, :], passed)
    high = passed.astype(BF).astype(F32)
    split_ref[0:4, :] = high
    split_ref[4:8, :] = passed - high

    def empty(d, carry):
        out_ref[d, :, 256:384] = jnp.zeros((16, 128), BF)
        return carry

    lax.fori_loop(0, 48, empty, 0, unroll=8)

    def leave(q, carry):
        parts = split_ref[:, quarter(q)]
        out_ref[48 + q, :, 256:384] = jnp.concatenate([parts[:, 0:128], parts[:, 128:256]], axis=0).astype(BF)
        return carry

    lax.fori_loop(0, 16, leave, 0, unroll=16)


def adam_kernel(parts_ref, chip_ref, owner_ref, out_ref, own_ref, other_ref, key_ref, old_ref):
    leaving = lax.axis_index("y") == 3
    core = lax.axis_index("core")
    totals = [jnp.zeros((16, 256), F32)] * 4
    for chip in range(64):
        kind = chip_class(chip)
        totals[kind] = totals[kind] + parts_ref[chip, :, 0:256].astype(F32)
    gradient = jnp.concatenate(totals, axis=1)

    @pl.when(leaving)
    def _():
        for y in (0, 2, 3):
            for q in range(16):
                parts = parts_ref[16 * y + q, :, 256:384].astype(F32)
                row = 4 * (q % 4)
                for h in range(2):
                    value = parts[8 * h : 8 * h + 4] + parts[8 * h + 4 : 8 * h + 8]
                    cut = slice((q // 4) * 256 + h * 128, (q // 4) * 256 + h * 128 + 128)
                    if y == 3:
                        old_ref[2, row : row + 4, cut] = value
                    else:
                        old_ref[0, row + y : row + y + 2, cut] = value[0:2]
                        old_ref[1, row + y : row + y + 2, cut] = value[2:4]

    @pl.when(jnp.logical_not(leaving))
    def _():
        for i in range(3):
            for n in range(16):
                k, u = n % 4, n // 4
                old_ref[i, 4 * k : 4 * k + 4, u * 256 : (u + 1) * 256] = chip_ref[
                    4 * i : 4 * i + 4, n * 256 : (n + 1) * 256
                ]

    new = adam_update(old_ref[0], old_ref[1], old_ref[2], gradient)
    own_ref[6:8, :] = jnp.zeros((2, HALF), F32)
    other_ref[6:8, :] = jnp.zeros((2, HALF), F32)
    values = [jnp.where(leaving, jnp.zeros_like(value), value) for value in new]
    for mine in range(2):

        @pl.when(core == mine)
        def _():
            for i in range(3):
                for n in range(16):
                    k, u = n % 4, n // 4
                    cut, lanes = slice(n * 256, (n + 1) * 256), slice(u * 256, (u + 1) * 256)
                    at = 4 * k + 2 * mine
                    own_ref[2 * i : 2 * i + 2, cut] = values[i][at : at + 2, lanes]
                    at = 4 * k + 2 * (1 - mine)
                    other_ref[2 * i : 2 * i + 2, cut] = values[i][at : at + 2, lanes]

    weights = new[0].astype(BF)

    for chip in range(64):
        kind = chip_class(chip)
        out_ref[chip, :, 0:256] = weights[:, kind * 256 : (kind + 1) * 256]

    lane, row = iota((64, 256), 1), iota((64, 256), 0)
    tiled = jnp.where((lane & 63) == row, 1.0, 0.0).astype(BF)
    across = pick(jnp.broadcast_to(owner_ref[...], (64, 64)).astype(F32).astype(BF), tiled)
    down = jnp.sum(jnp.where(lane == row, across, 0.0), axis=1, keepdims=True)
    earlier = (across == down) & (row < (lane & 63))
    slot = jnp.sum(jnp.where(earlier, 1.0, 0.0), axis=0, keepdims=True)
    key = (across[0:1, :] * 2.0 + slot).astype(jnp.int32) + 512 * (iota((1, 256), 1) >> 6)
    key_ref[...] = key
    moments = jnp.concatenate(
        [
            new[1 + part // 2][:, a * 256 + (part % 2) * 128 : a * 256 + (part % 2) * 128 + 128]
            for part in range(4)
            for a in range(4)
        ],
        axis=0,
    ).astype(BF)
    p = iota((1024, 256), 0)
    wanted = (p >> 4) * 4 + (p & 3) + 512 * ((p >> 2) & 3)
    chosen = jnp.where(key == wanted, 1.0, 0.0).astype(BF)
    out_ref[:, :, 256:384] = pick(chosen, moments).astype(BF).reshape(64, 16, 128)


def copy_kernel(blocks_ref, out_ref):
    out_ref[...] = blocks_ref[:, :, 0:256]


def place_half(views, key_ref, weights_ref, adopted_ref, adopted_at, adopted_ready, rows_ref, sems, core, side):
    blocks_ref = views[0][0]
    chip = own_chip()
    kind = chip_class(chip)
    low = iota((8, 256), 0) < 4

    def store(i):
        rows = pl.ds(pl.multiple_of(32 * i, 32), 32)
        return pltpu.make_async_copy(rows_ref.at[rows, :], weights_ref.at[rows, columns(side)], sems.at[i])

    def kept(i, carry):
        for axis in range(4):
            ref, lane = views[axis]
            for g in range(2):
                tiles = []
                for tile in range(2):
                    number = 8 * i + 4 * g + 2 * tile
                    even = ref[number, :, lane : lane + 256].astype(F32)
                    odd = ref[number + 1, :, lane : lane + 256].astype(F32)
                    cut = []
                    for s in (slice(0, 8), slice(8, 16)):
                        cut.append(jnp.where(low, even[s], turned(odd[s])))
                        cut.append(jnp.where(low, turned(even[s]), odd[s]))
                    tiles.append(cut)
                rows = pl.ds(pl.multiple_of(32 * i + 16 * g, 16), 16)
                for k in range(4):
                    rows_ref[rows, quarter((kind ^ axis) * 4 + k)] = jnp.concatenate(
                        [tiles[0][k], tiles[1][k]], axis=0
                    ).astype(BF)
        store(i).start()
        return carry

    for axis in range(4):
        ref, lane = views[axis]
        rows = pl.ds(pl.multiple_of(192 + 16 * (kind ^ axis), 16), 16)
        for q in range(16):
            rows_ref[rows, q * 256 : (q + 1) * 256] = ref[48 + q, :, lane : lane + 256]
    for i in range(6, 8):
        store(i).start()
    k = iota((8, 64), 0)
    wanted = jnp.where(k < 2, chip * 4 + core * 2 + k, -1)
    chosen = jnp.where(key_ref[:, 0:64] == wanted, 1.0, 0.0).astype(BF)
    masters = pick(chosen, rows_ref[192:256, :])
    adopted_ref[0, :, adopted_at(0, HALF)] = masters[0:2, :]
    moments = jnp.concatenate([blocks_ref[48 + q, :, 256:384] for q in range(16)], axis=1)
    for h in range(2):
        k = iota((8, 16), 0)
        found = pick(one_hot(jnp.where(k < 4, ((k >> 1) * 2 + h) * 4 + core * 2 + (k & 1), -1)), moments)
        for q in range(16):
            for i in range(2):
                adopted_ref[1 + i, :, adopted_at(q * 256 + h * 128, 128)] = found[
                    2 * i : 2 * i + 2, q * 128 : (q + 1) * 128
                ]
    adopted_ready()
    lax.fori_loop(0, 6, kept, 0, unroll=6)
    for i in range(8):
        store(i).wait()


def place_own_kernel(
    blocks_ref, x_ref, y_ref, z_ref, key_ref, weights_ref, adopted_ref, rows_ref, sems
):
    views = [(ref, 0) for ref in (blocks_ref, x_ref, y_ref, z_ref)]
    core = lax.axis_index("core")
    place_half(
        views, key_ref, weights_ref, adopted_ref, lambda start, size: slice(start, start + size), lambda: None,
        rows_ref, sems, core, core,
    )


def place_other_kernel(*refs):
    key_ref, _, half_ref, own_ref, other_ref = refs[4:9]
    weights_ref, adopted_out, kept_out, adopted_ref, kept_ref, rows_ref, sems, out_sems = refs[9:]
    views = [(ref, 0) for ref in refs[:4]]
    core = lax.axis_index("core")
    side = 1 - core
    kept_copy = pltpu.make_async_copy(kept_ref, kept_out, out_sems.at[0])
    adopted_copy = pltpu.make_async_copy(adopted_ref, adopted_out, out_sems.at[1])
    for i in range(3):
        adopted_ref[i, :, columns(core)] = half_ref[i]
        kept_ref[i, :, columns(core)] = own_ref[2 * i : 2 * i + 2, :]
        kept_ref[i, :, columns(side)] = other_ref[2 * i : 2 * i + 2, :]
    kept_copy.start()

    def at(start, size):
        return pl.ds(pl.multiple_of(side * HALF + start, 128), size)

    place_half(views, key_ref, weights_ref, adopted_ref, at, adopted_copy.start, rows_ref, sems, core, side)
    kept_copy.wait()
    adopted_copy.wait()


def params(mib=40):
    return pltpu.CompilerParams(vmem_limit_bytes=mib * 1024 * 1024)


def shape(dims, dtype):
    return jax.ShapeDtypeStruct(dims, dtype)


def swapped(value):
    return lax.ppermute(value, "core", [(0, 1), (1, 0)])


def to_neighbours(values):
    pairs = [(2 * p + c, 2 * ((p + 3 - 2 * c) % 4) + c) for p in range(4) for c in range(2)]
    return [lax.ppermute(value, (axis, "core"), pairs) for axis, value in zip("xyz", values)]


def from_leaving(value):
    pairs = [(96 + rank, 64 * (rank % 2) + rank) for rank in range(32)]
    return lax.ppermute(value, ("y", "z", "x", "core"), pairs)


def body(local_grads, master, first, second, new_owner):
    grads = local_grads.reshape(256, 8192)
    vmem = pl.BlockSpec(memory_space=pltpu.VMEM)
    hbm = pl.BlockSpec(memory_space=pltpu.HBM)
    core = lax.axis_index("core")
    got = swapped(lax.dynamic_slice(grads, (0, (1 - core) * HALF), (256, HALF)))
    stacked = pl.pallas_call(
        stack_kernel,
        in_specs=[vmem] * 2,
        out_specs=vmem,
        out_shape=shape((4, 8192), F32),
        compiler_params=params(),
        name="stack",
    )(master, first)
    passed = from_leaving(stacked)
    piece = shape((64, 16, 256), BF)
    keep, *to_send = pl.pallas_call(
        add_kernel,
        in_specs=[vmem] * 3,
        out_specs=[vmem] * 4,
        out_shape=[piece] * 4,
        compiler_params=params(),
        name="add_blocks",
    )(grads, got, passed)
    pair = pl.pallas_call(
        pair_kernel,
        in_specs=[vmem] * 4,
        out_specs=vmem,
        out_shape=shape((12, HALF), F32),
        compiler_params=params(),
        name="pair",
    )(master, first, second, passed)
    arrived = to_neighbours(to_send)
    pair = swapped(pair)
    partial, old = pl.pallas_call(
        merge_kernel,
        in_specs=[vmem] * 9,
        out_specs=[vmem] * 2,
        out_shape=[shape((64, 16, 384), BF), shape((16, HALF), F32)],
        scratch_shapes=[pltpu.VMEM((8, HALF), F32)],
        compiler_params=params(),
        name="merge",
    )(keep, *arrived, master, first, second, passed, pair)
    partial = lax.all_to_all(partial, CHIPS, 0, 0, tiled=True)
    payload, own_new, other_new, key = pl.pallas_call(
        adam_kernel,
        in_specs=[vmem] * 3,
        out_specs=[vmem] * 4,
        out_shape=[
            shape((64, 16, 384), BF),
            shape((8, HALF), F32),
            shape((8, HALF), F32),
            shape((1, 256), jnp.int32),
        ],
        scratch_shapes=[pltpu.VMEM((3, 16, 1024), F32)],
        compiler_params=params(),
        name="adam",
    )(partial, old, new_owner.reshape(1, 64))
    other_new = swapped(other_new)
    blocks = lax.all_to_all(payload, CHIPS, 0, 0, tiled=True)
    mine = pl.pallas_call(
        copy_kernel,
        in_specs=[vmem],
        out_specs=vmem,
        out_shape=piece,
        compiler_params=params(),
        name="mine",
    )(blocks)
    pieces = [blocks] + to_neighbours([mine] * 3)
    other_pieces = [swapped(value) for value in pieces]
    scratch = [pltpu.VMEM((256, HALF), BF), pltpu.SemaphoreType.DMA((8,))]
    weights, adopted = pl.pallas_call(
        place_own_kernel,
        in_specs=[vmem] * 5,
        out_specs=[hbm, vmem],
        out_shape=[shape((256, 8192), BF), shape((3, 2, HALF), F32)],
        scratch_shapes=scratch,
        compiler_params=params(),
        cost_estimate=pl.CostEstimate(flops=8_000_000, bytes_accessed=8_000_000, transcendentals=0),
        name="place_own",
    )(*pieces, key)
    weights, adopted, kept = pl.pallas_call(
        place_other_kernel,
        in_specs=[vmem] * 5 + [hbm] + [vmem] * 3,
        out_specs=[hbm] * 3,
        out_shape=[shape((256, 8192), BF), shape((3, 2, 8192), F32), shape((3, 2, 8192), F32)],
        scratch_shapes=[pltpu.VMEM((3, 2, 8192), F32)] * 2 + scratch + [pltpu.SemaphoreType.DMA((2,))],
        input_output_aliases={5: 0},
        compiler_params=params(),
        name="place_other",
    )(*other_pieces, key, weights, adopted, own_new, other_new)
    return (weights, kept.transpose(1, 0, 2), adopted.transpose(1, 0, 2)[None, None])


def solution(mesh):
    fine = Mesh(mesh.devices.reshape(4, 4, 4, 2), ("y", "z", "x", "core"))
    every = ("y", "z", "x", "core")
    in_specs = (P("y", ("z", "x", "core"), None, None), P(every, None), P(every, None), P(every, None), P())
    out_specs = (P(), P(every, None, None), P("y", ("z", "x", "core"), None, None, None))
    return jax.shard_map(body, mesh=fine, in_specs=in_specs, out_specs=out_specs, check_vma=False)
```
